256 devices in a mesh: req: 4 (over x_lo, core), patch: 64 (over y, z, x_hi).
Axes of the slice: x: 4 (x_hi: 2, x_lo: 2; x = x_hi * 2 + x_lo), y: 4, z: 8, core: 2. Of those that a mesh axis runs over, the one named last changes fastest.
Arguments:
- latent: bfloat16 [512, 128, 640], P(('req', 'patch')), parts along dimension 0, may hold values from -40 to 40, as said below
- gn_gain: float32 [640], replicated, may hold values from 0.25 to 1.75
- gn_bias: float32 [640], replicated, may hold values from -3 to 3
- conv_weight: bfloat16 [5760, 640], replicated, may hold values from -0.078125 to 0.078125
- conv_bias: float32 [640], replicated, may hold values from -3 to 3
- attn_gain: float32 [640], replicated, may hold values from 0.25 to 1.75
- attn_bias: float32 [640], replicated, may hold values from -3 to 3
- proj_in: bfloat16 [640, 640], replicated, may hold values from -0.25 to 0.25
- ln_gain: float32 [640], replicated, may hold values from 0.25 to 1.75
- qkv_weight: bfloat16 [640, 960], replicated, may hold values from -0.37890625 to 0.37890625
- out_weight: bfloat16 [320, 640], replicated, may hold values from -0.3125 to 0.3125
- proj_out: bfloat16 [640, 640], replicated, may hold values from -0.25 to 0.25
- stale_kv: bfloat16 [65536, 640], P(('req', 'patch')), parts along dimension 0, may hold values from -60 to 60
Outputs:
- block_out: bfloat16 [512, 128, 640], P(('req', 'patch')), parts along dimension 0
- fresh_kv: bfloat16 [65536, 640], P(('req', 'patch')), parts along dimension 0
The draws below stay inside these ranges and needn't reach their ends.
There are 4 independent parts, one for each index of `req`. The reference program is written for one: setup_inputs(seed, part) draws one part's arguments, and reference() takes and returns one part's arrays. A program takes and returns all parts, laid end to end along the dimension named above; an argument that names none is the same for every part. Nothing has to cross between parts.
Inputs may be any that keep to these rules, and one draw needn't show every extreme that they name: `latent`: activations with positions and channels scaled unevenly.
All inputs are finite; a program needn't handle non-finite values.
Results may differ from the reference program's by a relative error of at most 0.0085.
Values may be sent and summed in bfloat16 or wider, within the bound.
A program may use at most 128 MiB of HBM per device.

```python
import math
import jax
import jax.numpy as jnp
from jax import lax

C = 640
GROUPS = 32
HEADS = 5
HD = 64
WIDTH = 128
ROWS_DEV = 2
HEIGHT = 128
TOKENS = 16384
N_PATCH = 64


def draw_latent(key, part):
    key = jax.random.fold_in(key, 11)
    first, second, third, fourth = jax.random.split(key, 4)
    row_ids = jnp.arange(HEIGHT, dtype=jnp.float32) / max(HEIGHT - 1, 1)
    channel_scale = jnp.exp(jax.random.uniform(second, (C,), jnp.float32, math.log(0.5), math.log(2.0)))
    row_scale = jnp.exp(jax.random.uniform(third, (HEIGHT,), jnp.float32, math.log(0.35), math.log(2.0)))
    row_offset = jax.random.uniform(fourth, (HEIGHT,), jnp.float32, -1.0, 1.0)
    base = jnp.clip(jax.random.normal(first, (HEIGHT, WIDTH, C), jnp.float32), -3.0, 3.0)
    ramp = 1.0 + 2.0 * row_ids
    row_factor = ramp * row_scale
    values = base * row_factor[:, None, None] + row_offset[:, None, None]
    return (values * channel_scale).astype(jnp.bfloat16)


def draw_stale_kv(key, part):
    key = jax.random.fold_in(key, 23)
    first = jax.random.fold_in(key, 0)
    columns = 2 * HEADS * HD
    values = jnp.clip(jax.random.normal(first, (TOKENS, columns), jnp.float32), -6.0, 6.0) * 1.6
    return values.astype(jnp.bfloat16)


def centred(own_key, shape, scale, most, kind=jnp.bfloat16):
    values = scale * jax.random.normal(own_key, shape, jnp.float32)
    return jnp.clip(values, min=-most, max=most).astype(kind)


def setup_inputs(seed: int = 0, part: int = 0) -> dict:
    keys = jax.random.split(jax.random.key(seed), 14)
    part_keys = jax.random.split(jax.random.fold_in(keys[13], part), 14)
    return {
        "latent": draw_latent(jax.random.fold_in(jax.random.fold_in(keys[13], part), 71), part),
        "gn_gain": jnp.clip(1.0 + 0.15 * jax.random.normal(keys[1], (C,), jnp.float32), 0.25, 1.75),
        "gn_bias": centred(keys[2], (C,), 0.5, 3.0, jnp.float32),
        "conv_weight": centred(keys[3], (9 * C, C), (9 * C) ** -0.5, 0.078125),
        "conv_bias": centred(keys[4], (C,), 0.5, 3.0, jnp.float32),
        "attn_gain": jnp.clip(1.0 + 0.15 * jax.random.normal(keys[5], (C,), jnp.float32), 0.25, 1.75),
        "attn_bias": centred(keys[6], (C,), 0.5, 3.0, jnp.float32),
        "proj_in": centred(keys[7], (C, C), C ** -0.5, 0.25),
        "ln_gain": jnp.clip(1.0 + 0.15 * jax.random.normal(keys[8], (C,), jnp.float32), 0.25, 1.75),
        "qkv_weight": centred(keys[9], (C, 3 * HEADS * HD), (1.6 / C ** 0.5), 0.37890625),
        "out_weight": centred(keys[10], (HEADS * HD, C), (HEADS * HD) ** -0.5, 0.3125),
        "proj_out": centred(keys[11], (C, C), C ** -0.5, 0.25),
        "stale_kv": draw_stale_kv(jax.random.fold_in(jax.random.fold_in(keys[13], part), 71), part),
    }


def group_norm(values, gain, shift):
    flattened = values.reshape(-1, GROUPS, C // GROUPS)
    average = flattened.mean(axis=(0, 2), keepdims=True)
    centered = flattened - average
    spread = (centered * centered).mean(axis=(0, 2), keepdims=True)
    return (centered / jnp.sqrt(spread + 1e-05)).reshape(values.shape) * gain + shift

def reference(latent, gn_gain, gn_bias, conv_weight, conv_bias, attn_gain, attn_bias, proj_in, ln_gain, qkv_weight, out_weight, proj_out, stale_kv):
    widened = latent.astype(jnp.float32)
    activated = jax.nn.silu(group_norm(widened, gn_gain, gn_bias)).astype(jnp.bfloat16)
    padded = jnp.pad(activated, ((1, 1), (1, 1), (0, 0)))
    convolved = jnp.zeros((HEIGHT * WIDTH, C), jnp.float32)
    for tap_index in range(9):
        row_shift, col_shift = divmod(tap_index, 3)
        window = padded[row_shift:row_shift + HEIGHT, col_shift:col_shift + WIDTH].reshape(-1, C)
        convolved = convolved + jnp.dot(window, conv_weight[tap_index * C:(tap_index + 1) * C], preferred_element_type=jnp.float32)
    resid = (widened + convolved.reshape(HEIGHT, WIDTH, C) + conv_bias).astype(jnp.bfloat16)
    normed = group_norm(resid.astype(jnp.float32), attn_gain, attn_bias).astype(jnp.bfloat16).reshape(-1, C)
    inner = jnp.dot(normed, proj_in, preferred_element_type=jnp.float32)
    average = inner.mean(axis=-1, keepdims=True)
    deviation = inner - average
    spread = (deviation * deviation).mean(axis=-1, keepdims=True)
    lnorm = (deviation / jnp.sqrt(spread + 1e-05) * ln_gain).astype(jnp.bfloat16)
    mixed = jnp.dot(lnorm, qkv_weight, preferred_element_type=jnp.float32)
    heads_width = HEADS * HD
    queries = mixed[:, :heads_width].astype(jnp.bfloat16)
    fresh_kv = mixed[:, heads_width:].astype(jnp.bfloat16)
    band_tokens = ROWS_DEV * WIDTH
    score_scale = 1.0 / HD ** 0.5

    def one_band(band_index):
        start = (band_index * band_tokens).astype(jnp.int32)
        query_rows = lax.dynamic_slice_in_dim(queries, start, band_tokens, 0).astype(jnp.float32).reshape(band_tokens, HEADS, HD)
        own_fresh = lax.dynamic_slice_in_dim(fresh_kv, start, band_tokens, 0)
        keyset = lax.dynamic_update_slice_in_dim(stale_kv, own_fresh, start, 0)
        key_rows = keyset[:, :heads_width].astype(jnp.float32).reshape(-1, HEADS, HD)
        value_rows = keyset[:, heads_width:].astype(jnp.float32).reshape(-1, HEADS, HD)
        scores = jnp.einsum('qhd,khd->qhk', query_rows, key_rows) * score_scale
        largest = scores.max(axis=-1, keepdims=True)
        expos = jnp.exp(scores - largest)
        denominator = expos.sum(axis=-1)
        weights = expos.astype(jnp.bfloat16).astype(jnp.float32)
        summed = jnp.einsum('qhk,khd->qhd', weights, value_rows)
        return (summed / denominator[..., None]).reshape(band_tokens, heads_width).astype(jnp.bfloat16)
    attended = lax.map(one_band, jnp.arange(N_PATCH, dtype=jnp.int32)).reshape(-1, heads_width)
    hidden = (inner + jnp.dot(attended, out_weight, preferred_element_type=jnp.float32)).astype(jnp.bfloat16)
    final = jnp.dot(hidden, proj_out, preferred_element_type=jnp.float32).reshape(HEIGHT, WIDTH, C)
    block_out = (resid.astype(jnp.float32) + final).astype(jnp.bfloat16)
    return (block_out, fresh_kv)
```

```python
import functools

import jax
import jax.numpy as jnp
from jax import lax
from jax.experimental import pallas as pl
from jax.experimental.pallas import tpu as pltpu
from jax.sharding import PartitionSpec as P

C = 640
GROUPS = 32
PER_GROUP = C // GROUPS
HEADS = 5
HD = 64
WIDTH = 128
ROWS = 2
TOK = ROWS * WIDTH
HW = HEADS * HD
QL = 384
NY, NZ, NX = 4, 8, 2
NP = NY * NZ * NX
NG = NY * NX
KEYS = NZ * TOK
TILE = 1024
SCALE = (1.0 / HD**0.5) * 1.4426950408889634
F32 = jnp.float32
BF16 = jnp.bfloat16
HIGH = lax.Precision.HIGHEST


def place(y, z, x):
    return (lax.rem(y + NY, NY) * NZ + lax.rem(z + NZ, NZ)) * NX + lax.rem(x + NX, NX)


def remote(src, dst, send, recv, patch):
    return pltpu.make_async_remote_copy(
        src_ref=src,
        dst_ref=dst,
        send_sem=send,
        recv_sem=recv,
        device_id={"patch": patch},
        device_id_type=pl.DeviceIdType.MESH,
    )


def kernel(
    lat_hbm, gain1, bias1, convw_hbm, convb, gain2, bias2, pin_hbm, lng, qkvw_hbm, outw_hbm,
    pout_hbm, kv_hbm,
    out_ref, fresh_ref,
    lat, halo, convw, pin, qkvw, outw, pout, kv, vm, act, acc, resid, inner, gmat, gmat_t,
    stat_src, stat_buf, qbuf, sbuf, osend, orecv,
    lsem, kv_send, kv_recv, h_send, h_recv, st_send, st_recv, q_send, q_recv, o_send, o_recv,
):
    p = lax.axis_index("patch")
    y, z, x = p // (NZ * NX), lax.rem(p // NX, NZ), lax.rem(p, NX)

    loads = [
        pltpu.make_async_copy(lat_hbm.at[0], lat.at[pl.ds(0, WIDTH)], lsem.at[0]),
        pltpu.make_async_copy(lat_hbm.at[1], lat.at[pl.ds(WIDTH, WIDTH)], lsem.at[1]),
        pltpu.make_async_copy(convw_hbm, convw, lsem.at[2]),
        pltpu.make_async_copy(pin_hbm, pin, lsem.at[3]),
        pltpu.make_async_copy(qkvw_hbm, qkvw, lsem.at[4]),
        pltpu.make_async_copy(kv_hbm, kv.at[pl.ds(NZ * TOK, TOK)], lsem.at[5]),
        pltpu.make_async_copy(outw_hbm, outw.at[pl.ds(0, HW)], lsem.at[6]),
        pltpu.make_async_copy(pout_hbm, pout, lsem.at[7]),
    ]
    for c in loads:
        c.start()

    up, down = lax.rem(p + NP - 1, NP), lax.rem(p + 1, NP)
    zpeer = [place(y, z + d, x) for d in range(NZ)]
    gpeer = [place(y + k // NX, z, x + k % NX) for k in range(NG)]
    barrier = pltpu.get_barrier_semaphore()
    partners = zpeer[1:] + gpeer[1:] + [up, down]
    for q in partners:
        pl.semaphore_signal(
            barrier, inc=1, device_id={"patch": q}, device_id_type=pl.DeviceIdType.MESH
        )
    pl.semaphore_wait(barrier, len(partners))

    def block(rel, lo=0, n=TOK):
        return kv.at[pl.ds(rel * TOK + lo, n)]

    def kv_copy(way, s):
        lo, n = (0, TOK) if s < 3 else ((0, TOK // 2) if way == 0 else (TOK // 2, TOK // 2))
        rel = lambda t: NZ - 1 - t if way == 0 else t + 1
        src = kv_hbm if s == 0 else block(rel(s - 1), lo, n)
        return remote(
            src, block(rel(s), lo, n), kv_send.at[way, s], kv_recv.at[way, s],
            zpeer[1] if way == 0 else zpeer[NZ - 1],
        )

    ring = [[kv_copy(way, s) for s in range(4)] for way in range(2)]

    def kv_step(s):
        for way in range(2):
            if s > 0:
                ring[way][s - 1].wait_recv()
            if s < 4:
                ring[way][s].start()

    halos = [
        remote(lat_hbm.at[1], halo.at[pl.ds(0, WIDTH)], h_send.at[0], h_recv.at[0], down),
        remote(lat_hbm.at[0], halo.at[pl.ds(WIDTH, WIDTH)], h_send.at[1], h_recv.at[1], up),
    ]
    for c in halos:
        c.start()
    kv_step(0)

    ch = lax.broadcasted_iota(jnp.int32, (C, 128), 0)
    gr = lax.broadcasted_iota(jnp.int32, (C, 128), 1)
    gmat[...] = ((ch >= gr * PER_GROUP) & (ch < (gr + 1) * PER_GROUP)).astype(F32)
    ch = lax.broadcasted_iota(jnp.int32, (128, C), 1)
    gr = lax.broadcasted_iota(jnp.int32, (128, C), 0)
    gmat_t[...] = ((ch >= gr * PER_GROUP) & (ch < (gr + 1) * PER_GROUP)).astype(F32)
    row8 = lax.broadcasted_iota(jnp.int32, (8, 128), 0)

    def to_groups(v):
        return jnp.dot(v, gmat[...], precision=HIGH, preferred_element_type=F32)

    def to_channels(v):
        return jnp.dot(v, gmat_t[...], precision=HIGH, preferred_element_type=F32)

    stat_copies = []

    def statistics(ref, i):
        values = ref[...].astype(F32)
        total = jnp.broadcast_to(values.sum(axis=0, keepdims=True), (8, C))
        sums = to_groups(total)
        n = float(TOK * PER_GROUP)
        centred = values - to_channels(sums * (1.0 / n))[0:1]
        squares = to_groups(
            jnp.broadcast_to((centred * centred).sum(axis=0, keepdims=True), (8, C))
        )
        for rnd, peers in ((0, zpeer), (1, gpeer)):
            tile = jnp.where(row8 == 0, sums, squares)
            stat_src[i, rnd] = tile
            copies = [
                remote(
                    stat_src.at[i, rnd], stat_buf.at[i, rnd, k], st_send.at[i, rnd, k],
                    st_recv.at[i, rnd, k], peers[k],
                )
                for k in range(1, 8)
            ]
            for c in copies:
                c.start()
            for c in copies:
                c.wait_recv()
            stat_copies.extend(copies)
            parts = [tile] + [stat_buf[i, rnd, k] for k in range(1, 8)]
            s = [t[0:1] for t in parts]
            total = functools.reduce(jnp.add, s)
            mean = total * (1.0 / (8 * n))
            spread = functools.reduce(
                jnp.add, [t[1:2] + (a * (1.0 / n) - mean) ** 2 * n for t, a in zip(parts, s)]
            )
            sums = jnp.broadcast_to(total, (8, 128))
            squares = jnp.broadcast_to(spread, (8, 128))
            n = n * 8
        rstd = lax.rsqrt(squares * (1.0 / n) + 1e-05)
        wide = to_channels(jnp.where(row8 == 0, sums * (1.0 / n), rstd))
        return wide[0:1], wide[1:2]

    loads[0].wait()
    loads[1].wait()
    mean, rstd = statistics(lat, 0)
    kv_step(1)

    scale = rstd * gain1[...]
    for c in halos:
        c.wait_recv()
    col = lax.broadcasted_iota(jnp.int32, (WIDTH, C), 0)
    for r in range(ROWS + 2):
        if r == 0:
            v = halo[0:WIDTH]
        elif r == ROWS + 1:
            v = halo[WIDTH : 2 * WIDTH]
        else:
            v = lat[(r - 1) * WIDTH : r * WIDTH]
        v = (v.astype(F32) - mean) * scale + bias1[...]
        v = v / (1.0 + jnp.exp(-v))
        if r == 0:
            v = jnp.where(p == 0, 0.0, v)
        elif r == ROWS + 1:
            v = jnp.where(p == NP - 1, 0.0, v)
        rows = pl.ds(r * WIDTH, WIDTH)
        act[rows, 0:C] = jnp.where(col == 0, 0.0, pltpu.roll(v, 1, 0)).astype(BF16)
        act[rows, C : 2 * C] = v.astype(BF16)
        act[rows, 2 * C : 3 * C] = jnp.where(
            col == WIDTH - 1, 0.0, pltpu.roll(v, WIDTH - 1, 0)
        ).astype(BF16)

    loads[2].wait()
    for r in range(3):
        d = jnp.dot(
            act[r * WIDTH : r * WIDTH + TOK, :],
            convw[r * 3 * C : (r + 1) * 3 * C, :],
            preferred_element_type=F32,
        )
        if r == 0:
            acc[...] = d
        elif r == 1:
            acc[...] += d
            kv_step(2)
        else:
            resid[...] = (lat[...].astype(F32) + (acc[...] + d) + convb[...]).astype(BF16)

    mean, rstd = statistics(resid, 1)
    kv_step(3)
    scale = rstd * gain2[...]
    normed = ((resid[...].astype(F32) - mean) * scale + bias2[...]).astype(BF16)
    loads[3].wait()
    inner[...] = jnp.dot(normed, pin[...], preferred_element_type=F32)
    v = inner[...]
    v = v - v.mean(axis=1, keepdims=True)
    v = v * lax.rsqrt((v * v).mean(axis=1, keepdims=True) + 1e-05) * lng[...]
    loads[4].wait()
    mixed = jnp.dot(v.astype(BF16), qkvw[...], preferred_element_type=F32)
    qbuf[0] = mixed[:, 0:QL].astype(BF16)
    q_copies = [
        remote(qbuf.at[0], qbuf.at[k], q_send.at[k], q_recv.at[k], gpeer[k]) for k in range(1, NG)
    ]
    for c in q_copies:
        c.start()
    fresh = mixed[:, HW:].astype(BF16)
    fresh_ref[...] = fresh
    kv[0:TOK] = fresh
    kv_step(4)
    loads[5].wait()

    lane = lax.broadcasted_iota(jnp.int32, (TOK, 128), 1)
    low = lane < HD

    def widen(b, carry):
        rows = pl.ds(pl.multiple_of(b * TOK, TOK), TOK)
        for h in range(HEADS):
            t = 2 + (h + 1) // 2
            v = kv[rows, t * 128 : (t + 1) * 128].astype(F32)
            own = low if h % 2 else ~low
            vm[h, rows, :] = jnp.where(own, v, 1.0).astype(BF16)
        return carry

    lax.fori_loop(0, NZ + 1, widen, 0)

    def attend(k, carry):
        @pl.when(k > 0)
        def _():
            remote(
                qbuf.at[k], qbuf.at[k], q_send.at[k], q_recv.at[k], gpeer[1]
            ).wait_recv()

        start = pl.multiple_of(jnp.where(k == 0, 0, TOK), TOK)

        def query(h):
            t = h // 2
            q = qbuf[k, :, t * 128 : (t + 1) * 128].astype(F32)
            return jnp.where(~low if h % 2 else low, q, 0.0).astype(BF16)

        def score(q, h, t):
            keys = kv[
                pl.ds(pl.multiple_of(start + t * TILE, TOK), TILE),
                (h // 2) * 128 : (h // 2 + 1) * 128,
            ]
            return lax.dot_general(
                q, keys, (((1,), (1,)), ((), ())), preferred_element_type=F32
            )

        def largest(m, s):
            for j in range(TILE // 128):
                part = s[:, j * 128 : (j + 1) * 128]
                m = part if m is None else jnp.maximum(m, part)
            return m

        tiles = KEYS // TILE
        q = query(0)
        top = None
        for t in range(tiles):
            s = score(q, 0, t)
            sbuf[0, :, t * TILE : (t + 1) * TILE] = s
            top = largest(top, s)
        stats = jnp.zeros((TOK, 128), F32)
        even = None
        for h in range(HEADS):
            m = jnp.max(top, axis=1, keepdims=True) * SCALE
            top = None
            o = None
            if h + 1 < HEADS:
                q = query(h + 1)
            for t in range(tiles):
                cols = slice(t * TILE, (t + 1) * TILE)
                if h + 1 < HEADS:
                    s = score(q, h + 1, t)
                    sbuf[(h + 1) % 2, :, cols] = s
                    top = largest(top, s)
                w = jnp.exp2(sbuf[h % 2, :, cols] * SCALE - m).astype(BF16)
                d = jnp.dot(
                    w,
                    vm[h, pl.ds(pl.multiple_of(start + t * TILE, TOK), TILE), :],
                    preferred_element_type=F32,
                )
                o = d if o is None else o + d
            turned = pltpu.roll(o, HD, 1)
            ratio = turned / o
            stats = jnp.where(lane == HD + h, jnp.log2(o if h % 2 else turned) + m, stats)
            if h % 2:
                t = h // 2
                osend[k, :, t * 128 : (t + 1) * 128] = jnp.where(low, even, ratio).astype(BF16)
            else:
                even = ratio
        first = stats.astype(BF16).astype(F32)
        rest = stats - first
        second = rest.astype(BF16).astype(F32)
        third = rest - second
        tail = jnp.where(
            lane < HD + 8,
            first,
            jnp.where(lane < HD + 16, pltpu.roll(second, 8, 1), pltpu.roll(third, 16, 1)),
        )
        osend[k, :, 2 * 128 : 3 * 128] = jnp.where(low, even, tail).astype(BF16)

        @pl.when(k > 0)
        def _():
            owner = place(y - k // NX, z, x - lax.rem(k, NX))
            remote(osend.at[k], orecv.at[k], o_send.at[k], o_recv.at[k], owner).start()

        return carry

    lax.fori_loop(0, NG, attend, 0)

    loads[6].wait()
    loads[7].wait()
    outw[HW:QL] = jnp.zeros((QL - HW, C), BF16)
    for k in range(1, NG):
        remote(osend.at[k], orecv.at[k], o_send.at[k], o_recv.at[k], gpeer[k]).wait_recv()

    def part(k):
        return osend[0] if k == 0 else orecv[k]

    logs = []
    for k in range(NG):
        t = part(k)[:, 256:384].astype(F32)
        logs.append(t + pltpu.roll(t, 128 - 8, 1) + pltpu.roll(t, 128 - 16, 1))
    top = functools.reduce(jnp.maximum, logs)
    valid = (lane >= HD) & (lane < HD + HEADS)
    shares = [jnp.where(valid, jnp.exp2(t - top), 0.0) for t in logs]
    whole = functools.reduce(jnp.add, shares)
    inverse = 1.0 / jnp.where(valid, whole, 1.0)
    hrow = lax.broadcasted_iota(jnp.int32, (128, QL), 0)
    hcol = lax.broadcasted_iota(jnp.int32, (128, QL), 1)
    head = jnp.where(hrow < HD + 8, hrow - HD, hrow - HD - 8)
    spread = (
        (head >= 0) & (head < HEADS) & (hcol >= head * HD) & (hcol < (head + 1) * HD)
    ).astype(F32).astype(BF16)
    joined = jnp.zeros((TOK, QL), F32)
    for k in range(NG):
        w = shares[k] * inverse
        hi = w.astype(BF16).astype(F32)
        w = (hi + pltpu.roll(w - hi, 8, 1)).astype(BF16)
        joined = joined + jnp.dot(w, spread, preferred_element_type=F32) * part(k).astype(F32)
    hidden = inner[...] + jnp.dot(joined.astype(BF16), outw[...], preferred_element_type=F32)
    final = jnp.dot(hidden.astype(BF16), pout[...], preferred_element_type=F32)
    final = (resid[...].astype(F32) + final).astype(BF16)
    out_ref[0] = final[0:WIDTH]
    out_ref[1] = final[WIDTH:TOK]

    for way in range(2):
        for s in range(4):
            ring[way][s].wait_send()
    for c in halos + stat_copies + q_copies:
        c.wait_send()
    for k in range(1, NG):
        remote(osend.at[k], orecv.at[k], o_send.at[k], o_recv.at[k], gpeer[k]).wait_send()


def local(
    latent, gn_gain, gn_bias, conv_weight, conv_bias, attn_gain, attn_bias, proj_in, ln_gain,
    qkv_weight, out_weight, proj_out, stale_kv,
):
    hbm = pl.BlockSpec(memory_space=pl.ANY)
    vmem = pl.BlockSpec(memory_space=pltpu.VMEM)
    row = lambda v: v.reshape(1, C)
    dma = pltpu.SemaphoreType.DMA
    return pl.pallas_call(
        kernel,
        out_shape=(
            jax.ShapeDtypeStruct((ROWS, WIDTH, C), BF16),
            jax.ShapeDtypeStruct((TOK, 2 * HW), BF16),
        ),
        in_specs=[hbm, vmem, vmem, hbm, vmem, vmem, vmem, hbm, vmem, hbm, hbm, hbm, hbm],
        out_specs=(vmem, vmem),
        scratch_shapes=[
            pltpu.VMEM((TOK, C), BF16),
            pltpu.VMEM((2 * WIDTH, C), BF16),
            pltpu.VMEM((9 * C, C), BF16),
            pltpu.VMEM((C, C), BF16),
            pltpu.VMEM((C, 3 * HW), BF16),
            pltpu.VMEM((QL, C), BF16),
            pltpu.VMEM((C, C), BF16),
            pltpu.VMEM(((NZ + 1) * TOK, 2 * HW), BF16),
            pltpu.VMEM((HEADS, (NZ + 1) * TOK, 128), BF16),
            pltpu.VMEM(((ROWS + 2) * WIDTH, 3 * C), BF16),
            pltpu.VMEM((TOK, C), F32),
            pltpu.VMEM((TOK, C), BF16),
            pltpu.VMEM((TOK, C), F32),
            pltpu.VMEM((C, 128), F32),
            pltpu.VMEM((128, C), F32),
            pltpu.VMEM((2, 2, 8, 128), F32),
            pltpu.VMEM((2, 2, 8, 8, 128), F32),
            pltpu.VMEM((NG, TOK, QL), BF16),
            pltpu.VMEM((2, TOK, KEYS), F32),
            pltpu.VMEM((NG, TOK, QL), BF16),
            pltpu.VMEM((NG, TOK, QL), BF16),
            dma((8,)), dma((2, 4)), dma((2, 4)), dma((2,)), dma((2,)),
            dma((2, 2, 8)), dma((2, 2, 8)), dma((NG,)), dma((NG,)), dma((NG,)), dma((NG,)),
        ],
        compiler_params=pltpu.CompilerParams(
            collective_id=0, has_side_effects=True, vmem_limit_bytes=56 * 2**20
        ),
    )(
        latent, row(gn_gain), row(gn_bias), conv_weight, row(conv_bias), row(attn_gain),
        row(attn_bias), proj_in, row(ln_gain), qkv_weight, out_weight, proj_out, stale_kv,
    )


def solution(mesh):
    in_specs = (P(("req", "patch"), None, None),) + (P(),) * 11 + (P(("req", "patch"), None),)
    out_specs = (P(("req", "patch"), None, None), P(("req", "patch"), None))
    return jax.shard_map(local, mesh=mesh, in_specs=in_specs, out_specs=out_specs, check_vma=False)
```

```python
import functools

import jax
import jax.numpy as jnp
from jax import lax
from jax.experimental import pallas as pl
from jax.experimental.pallas import tpu as pltpu
from jax.sharding import PartitionSpec as P

C = 640
GROUPS = 32
PER_GROUP = C // GROUPS
HEADS = 5
HD = 64
WIDTH = 128
ROWS = 2
TOK = ROWS * WIDTH
HW = HEADS * HD
QL = 384
NY, NZ, NX = 4, 8, 2
NP = NY * NZ * NX
NG = NY
NK = NZ * NX
KEYS = NK * TOK
TILE = 1024
SCALE = (1.0 / HD**0.5) * 1.4426950408889634
F32 = jnp.float32
BF16 = jnp.bfloat16
OFFSETS = (0, 1, 3, 2)
PARTS = ((4,), (0, 1), (2, 3))
UNITS = (2, 2, 2)


def place(y, z, x):
    return (lax.rem(y + NY, NY) * NZ + lax.rem(z + NZ, NZ)) * NX + lax.rem(x + NX, NX)


def remote(src, dst, send, recv, patch):
    return pltpu.make_async_remote_copy(
        src_ref=src,
        dst_ref=dst,
        send_sem=send,
        recv_sem=recv,
        device_id={"patch": patch},
        device_id_type=pl.DeviceIdType.MESH,
    )


def kernel(
    lat_hbm, gain1, bias1, convw_hbm, convb, gain2, bias2, pin_hbm, lng, qkvw_hbm, outw_hbm,
    pout_hbm, kv_hbm,
    out_ref, fresh_ref,
    lat, halo, convw, pin, qkvw, outw, pout, kv0, kv1, kv2, own, vm, act, acc, resid, inner, gmat, gmat_t,
    stat_src, stat_buf, q0, q1, q2, sbuf, logs_ref, os0, os1, os2, or0, or1, or2,
    lsem, kv_send, kv_recv, own_send, own_recv, x_send, x_recv, h_send, h_recv, st_send, st_recv, q_send, q_recv, o_send, o_recv,
):
    p = lax.axis_index("patch")
    y, z, x = p // (NZ * NX), lax.rem(p // NX, NZ), lax.rem(p, NX)

    loads = [
        pltpu.make_async_copy(lat_hbm.at[0], lat.at[pl.ds(0, WIDTH)], lsem.at[0]),
        pltpu.make_async_copy(lat_hbm.at[1], lat.at[pl.ds(WIDTH, WIDTH)], lsem.at[1]),
        pltpu.make_async_copy(kv_hbm, own, lsem.at[2]),
        pltpu.make_async_copy(convw_hbm, convw, lsem.at[3]),
        pltpu.make_async_copy(pin_hbm, pin, lsem.at[4]),
        pltpu.make_async_copy(qkvw_hbm, qkvw, lsem.at[5]),
        pltpu.make_async_copy(outw_hbm, outw.at[pl.ds(0, HW)], lsem.at[6]),
        pltpu.make_async_copy(pout_hbm, pout, lsem.at[7]),
    ]
    for c in loads:
        c.start()

    parts = (kv0, kv1, kv2)

    def pack(block, keys, values):
        rows = pl.ds(block * TOK, TOK)
        for c in (1, 2):
            parts[c][rows, 0:128] = keys[:, (c - 1) * 128 : c * 128]
            parts[c][rows, 128:256] = values[:, (c - 1) * 128 : c * 128]
        kv0[rows, 0:64] = keys[:, 256:320]
        kv0[rows, 64:128] = values[:, 256:320]

    loads[2].wait()
    pack(NK, own[:, 0:HW], own[:, HW : 2 * HW])

    up, down = lax.rem(p + NP - 1, NP), lax.rem(p + 1, NP)
    zpeer = [place(y, z + d, x) for d in range(NZ)]
    gpeer = [place(y + dy, z, x) for dy in OFFSETS]
    wpeer = [place(y + k // NX, z, x + k % NX) for k in range(NY * NX)]
    barrier = pltpu.get_barrier_semaphore()
    partners = zpeer[1:] + wpeer[1:] + [up, down]
    for q in partners:
        pl.semaphore_signal(
            barrier, inc=1, device_id={"patch": q}, device_id_type=pl.DeviceIdType.MESH
        )

    ch = lax.broadcasted_iota(jnp.int32, (C, 128), 0)
    gr = lax.broadcasted_iota(jnp.int32, (C, 128), 1)
    gmat[...] = ((ch >= gr * PER_GROUP) & (ch < (gr + 1) * PER_GROUP)).astype(F32).astype(BF16)
    ch = lax.broadcasted_iota(jnp.int32, (128, C), 1)
    gr = lax.broadcasted_iota(jnp.int32, (128, C), 0)
    gmat_t[...] = ((ch >= gr * PER_GROUP) & (ch < (gr + 1) * PER_GROUP)).astype(F32).astype(BF16)

    def three(v, row, out):
        at = lax.broadcasted_iota(jnp.int32, out.shape, 0)
        for t in range(3):
            short = v.astype(BF16).astype(F32)
            out = jnp.where(at == row + t, short, out)
            v = v - short
        return out

    def to_groups(v):
        r = jnp.dot(
            three(v, 0, jnp.zeros((16, C), F32)).astype(BF16), gmat[...], preferred_element_type=F32
        )
        return r[0:1] + r[1:2] + r[2:3]

    def to_channels(v, w):
        r = three(w, 3, three(v, 0, jnp.zeros((16, 128), F32)))
        r = jnp.dot(r.astype(BF16), gmat_t[...], preferred_element_type=F32)
        return r[0:1] + r[1:2] + r[2:3], r[3:4] + r[4:5] + r[5:6]

    stat_copies = []

    low_groups = lax.broadcasted_iota(jnp.int32, (1, 128), 1) < GROUPS

    def local_sums(ref):
        values = ref[...].astype(F32)
        sums = to_groups(values.sum(axis=0, keepdims=True))
        middle = sums * (1.0 / (TOK * PER_GROUP))
        centred = values - to_channels(middle, middle)[0]
        return sums, to_groups((centred * centred).sum(axis=0, keepdims=True))

    def statistics(found, i, steps):
        sums, squares = found
        n = float(TOK * PER_GROUP)
        for rnd, peers in ((0, zpeer), (1, wpeer)):
            tile = jnp.where(low_groups, sums, pltpu.roll(squares, GROUPS, 1))
            stat_src[i, rnd, 0:1] = tile
            copies = [
                remote(
                    stat_src.at[i, rnd, pl.ds(0, 1)], stat_buf.at[i, rnd, k, pl.ds(0, 1)],
                    st_send.at[i, rnd, k], st_recv.at[i, rnd, k], peers[k],
                )
                for k in range(1, 8)
            ]
            for c in copies:
                c.start()
            for c, t in steps[rnd]:
                kv_step(c, t)
            for c in copies:
                c.wait_recv()
            stat_copies.extend(copies)
            parts = [tile] + [stat_buf[i, rnd, k, 0:1] for k in range(1, 8)]
            total = functools.reduce(jnp.add, parts)
            mean = total * (1.0 / (8 * n))
            spread = functools.reduce(
                jnp.add,
                [pltpu.roll(t, 128 - GROUPS, 1) + (t * (1.0 / n) - mean) ** 2 * n for t in parts],
            )
            sums = jnp.where(low_groups, total, 0.0)
            squares = jnp.where(low_groups, spread, 0.0)
            n = n * 8
        return to_channels(sums * (1.0 / n), lax.rsqrt(squares * (1.0 / n) + 1e-05))

    loads[0].wait()
    loads[1].wait()
    found = local_sums(lat)
    pl.semaphore_wait(barrier, len(partners))

    def ahead(way, s):
        if s < 0:
            return NZ
        return NZ - 1 - s if way == 0 else s + 1

    def cut(s, way, n):
        return (0, n) if s < 3 else ((0, n // 2) if way == 0 else (n // 2, n // 2))

    def rows_of(c, r, lo, n):
        return parts[c].at[pl.ds((2 * r - (c < 2)) * TOK + lo, n)]

    def kv_copy(c, way, s):
        lo, n = cut(s, way, 2 * TOK if c < 2 and s > 0 else TOK)
        return remote(
            rows_of(c, ahead(way, s - 1), lo, n), rows_of(c, ahead(way, s), lo, n),
            kv_send.at[c, way, s], kv_recv.at[c, way, s], zpeer[1] if way == 0 else zpeer[NZ - 1],
        )

    def own_copy(c, way):
        return remote(
            parts[c].at[pl.ds(2 * NZ * TOK, TOK)],
            parts[c].at[pl.ds(2 * ahead(way, 0) * TOK, TOK)],
            own_send.at[c, way], own_recv.at[c, way], zpeer[1] if way == 0 else zpeer[NZ - 1],
        )

    def across(c, way, s):
        lo, n = cut(s, way, TOK)
        at = 2 * ahead(way, s) * TOK + lo
        return remote(
            parts[c].at[pl.ds(at, n)], parts[c].at[pl.ds(at - TOK, n)],
            x_send.at[c, way, s + 1], x_recv.at[c, way, s + 1], wpeer[1],
        )

    ring = [[[kv_copy(c, way, s) for s in range(4)] for way in range(2)] for c in range(3)]
    owns = [[own_copy(c, way) for way in range(2)] for c in range(2)]
    cross = [[across(c, 0, -1)] for c in range(3)]
    cross[2] += [across(2, way, s) for s in range(4) for way in range(2)]

    def kv_step(c, s):
        if c < 2 and s == 0:
            cross[c][0].wait_recv()
        for way in range(2):
            if s > 0:
                ring[c][way][s - 1].wait_recv()
                if c < 2 and s == 1:
                    owns[c][way].wait_recv()
                if c == 2:
                    cross[c][1 + 2 * (s - 1) + way].start()
            if s < 4:
                ring[c][way][s].start()

    def kv_end():
        for copy in cross[2]:
            copy.wait_recv()

    halos = [
        remote(lat_hbm.at[1], halo.at[pl.ds(0, WIDTH)], h_send.at[0], h_recv.at[0], down),
        remote(lat_hbm.at[0], halo.at[pl.ds(WIDTH, WIDTH)], h_send.at[1], h_recv.at[1], up),
    ]
    cross[0][0].start()
    for c in owns[0] + owns[1]:
        c.start()
    kv_step(2, 0)
    cross[1][0].start()
    for c in halos:
        c.start()
    cross[2][0].start()
    mean, rstd = statistics(found, 0, ((), ((0, 0), (1, 0))))

    scale = rstd * gain1[...].reshape(1, C)
    shift = bias1[...].reshape(1, C)
    col = lax.broadcasted_iota(jnp.int32, (WIDTH, C), 0)

    def activate(r):
        if r == 0:
            v = halo[0:WIDTH]
        elif r == ROWS + 1:
            v = halo[WIDTH : 2 * WIDTH]
        else:
            v = lat[(r - 1) * WIDTH : r * WIDTH]
        v = (v.astype(F32) - mean) * scale + shift
        v = v / (1.0 + jnp.exp(-v))
        if r == 0:
            v = jnp.where(p == 0, 0.0, v)
        elif r == ROWS + 1:
            v = jnp.where(p == NP - 1, 0.0, v)
        rows = pl.ds(r * WIDTH, WIDTH)
        act[rows, 0:C] = jnp.where(col == 0, 0.0, pltpu.roll(v, 1, 0)).astype(BF16)
        act[rows, C : 2 * C] = v.astype(BF16)
        act[rows, 2 * C : 3 * C] = jnp.where(
            col == WIDTH - 1, 0.0, pltpu.roll(v, WIDTH - 1, 0)
        ).astype(BF16)

    def convolve(r):
        return jnp.dot(
            act[r * WIDTH : r * WIDTH + TOK, :],
            convw[r * 3 * C : (r + 1) * 3 * C, :],
            preferred_element_type=F32,
        )

    activate(1)
    activate(2)
    loads[3].wait()
    kv_step(0, 1)
    acc[...] = convolve(1)
    kv_step(2, 1)
    for c in halos:
        c.wait_recv()
    activate(0)
    activate(3)
    acc[...] += convolve(0)
    resid[...] = (
        lat[...].astype(F32) + (acc[...] + convolve(2)) + convb[...].reshape(1, C)
    ).astype(BF16)

    kv_step(1, 1)
    mean, rstd = statistics(local_sums(resid), 1, (((0, 2),), ((2, 2),)))
    scale = rstd * gain2[...].reshape(1, C)
    normed = ((resid[...].astype(F32) - mean) * scale + bias2[...].reshape(1, C)).astype(BF16)
    loads[4].wait()
    inner[...] = jnp.dot(normed, pin[...], preferred_element_type=F32)
    v = inner[...]
    v = v - v.mean(axis=1, keepdims=True)
    v = v * lax.rsqrt((v * v).mean(axis=1, keepdims=True) + 1e-05) * lng[...].reshape(1, C)
    loads[5].wait()
    lnorm = v.astype(BF16)
    kv_step(0, 3)
    kv_step(1, 2)

    def project(first):
        return lax.dot_general(
            lnorm, qkvw[first : first + HW], (((1,), (1,)), ((), ())), preferred_element_type=F32
        ).astype(BF16)

    qs, oss, ors = (q0, q1, q2), (os0, os1, os2), (or0, or1, or2)

    def send_queries(c, k, patch):
        remote(qs[c].at[0], qs[c].at[k], q_send.at[c, k], q_recv.at[c, k], patch).start()

    queries = project(0)
    q0[0, :, 0:64] = queries[:, 256:320]
    q0[0, :, 64:128] = jnp.zeros((TOK, 64), BF16)
    for c in (1, 2):
        qs[c][0] = queries[:, (c - 1) * 128 : c * 128]
    for c in range(3):
        for k in range(1, NG):
            send_queries(c, k, gpeer[k])
    keys, values = project(HW), project(2 * HW)
    fresh_ref[:, 0:HW] = keys
    fresh_ref[:, HW : 2 * HW] = values
    pack(0, keys, values)

    lane = lax.broadcasted_iota(jnp.int32, (TOK, 128), 1)
    low = lane < HD

    def widen(c, first, last):
        def one(b, carry):
            rows = pl.ds(pl.multiple_of(b * TOK, TOK), TOK)
            for i, h in enumerate(PARTS[c]):
                v = parts[c][rows, 128:256] if c > 0 else kv0[rows, :]
                upper = i == 1 or c == 0
                vm[h, rows, :] = jnp.where(~low if upper else low, v.astype(F32), 1.0).astype(BF16)
            return carry

        lax.fori_loop(first, last, one, 0)

    tiles = KEYS // TILE

    def attend(c, slots, before, after):
        def begin(k):
            return pl.multiple_of(jnp.where(k == 0, 0, TOK), TOK)

        def query(k, i):
            q = qs[c][k].astype(F32)
            return jnp.where(~low if i else low, q, 0.0).astype(BF16)

        def score(q, k, t):
            keys = parts[c][pl.ds(pl.multiple_of(begin(k) + t * TILE, TOK), TILE), 0:128]
            return lax.dot_general(q, keys, (((1,), (1,)), ((), ())), preferred_element_type=F32)

        def largest(m, s):
            for j in range(TILE // 128):
                part = s[:, j * 128 : (j + 1) * 128]
                m = part if m is None else jnp.maximum(m, part)
            return m

        work = [(k, i) for k in slots for i in range(len(PARTS[c]))]
        before(0)
        q = query(*work[0])
        top = None
        for t in range(tiles):
            s = score(q, slots[0], t)
            sbuf[0, :, t * TILE : (t + 1) * TILE] = s
            top = largest(top, s)
        ratios, stats = [], None
        for n, (k, i) in enumerate(work):
            h = PARTS[c][i]
            m = jnp.max(top, axis=1, keepdims=True) * SCALE
            top = None
            o = None
            following = work[n + 1] if n + 1 < len(work) else None
            if following:
                if following[1] == 0:
                    before((n + 1) // len(PARTS[c]))
                q = query(*following)
            for t in range(tiles):
                cols = slice(t * TILE, (t + 1) * TILE)
                if following:
                    s = score(q, following[0], t)
                    sbuf[(n + 1) % 2, :, cols] = s
                    top = largest(top, s)
                w = jnp.exp2(sbuf[n % 2, :, cols] * SCALE - m).astype(BF16)
                d = jnp.dot(
                    w,
                    vm[h, pl.ds(pl.multiple_of(begin(k) + t * TILE, TOK), TILE), :],
                    preferred_element_type=F32,
                )
                o = d if o is None else o + d
            turned = pltpu.roll(o, HD, 1)
            ratio = turned / o if c == 0 else o / turned
            log = jnp.log2(turned if i == 1 or c == 0 else o) + m
            ratios.append(ratio)
            stats = jnp.where(lane == HD + h, log, 0.0 if stats is None else stats)
            if i + 1 == len(PARTS[c]):
                after(n // len(PARTS[c]), k, ratios, stats)
                ratios, stats = [], None

    def behind(k, sign):
        dy = jnp.where(k == 1, 1, jnp.where(k == 2, 3, jnp.where(k == 3, 2, 0)))
        return place(y + sign * dy, z, x)

    def give_back(c, k):
        remote(
            oss[c].at[k], ors[c].at[k], o_send.at[c, k], o_recv.at[c, k], behind(k, -1)
        ).start()

    def await_queries(c, k):
        remote(qs[c].at[0], qs[c].at[k], q_send.at[c, k], q_recv.at[c, k], gpeer[1]).wait_recv()

    def step(c, b, unit):
        slots = [b * unit + u if c < 2 else NG - 1 - (b * unit + u) for u in range(unit)]

        def before(u):
            if u > 0 if c < 2 else u + 1 < unit:
                await_queries(c, slots[u])
            else:
                pl.when(slots[u] > 0)(lambda: await_queries(c, slots[u]))

        def after(u, k, ratios, stats):
            if c == 0:
                oss[0][k] = ratios[0].astype(BF16)
                logs_ref[k] = stats
                return
            oss[c][k] = jnp.where(low, ratios[0], ratios[1]).astype(BF16)
            if c == 1:
                logs_ref[k] += stats
                return
            stats = logs_ref[k] + stats
            first = stats.astype(BF16).astype(F32)
            rest = stats - first
            second = rest.astype(BF16).astype(F32)
            third = rest - second
            tail = jnp.where(
                lane < HD + 8,
                first,
                jnp.where(lane < HD + 16, pltpu.roll(second, 8, 1), pltpu.roll(third, 16, 1)),
            )
            os0[k] = jnp.where(low, os0[k].astype(F32), tail).astype(BF16)
            if u + 1 < unit:
                give_back(2, k)
                give_back(0, k)

        attend(c, slots, before, after)
        if c > 0:
            for u in range(unit):
                if c == 1 and u > 0:
                    give_back(1, slots[u])
                elif c == 1 or u + 1 == unit:

                    @pl.when(slots[u] > 0)
                    def _():
                        give_back(c, slots[u])
                        if c == 2:
                            give_back(0, slots[u])

    kv_step(2, 3)
    kv_step(0, 4)
    widen(0, 0, NK + 1)

    def part0(b, carry):
        pl.when(b == 1)(lambda: kv_step(1, 3))
        step(0, b, UNITS[0])
        return carry

    def part1(b, carry):
        step(1, b, UNITS[1])
        return carry

    def part2(b, carry):
        step(2, b, UNITS[2])
        return carry

    lax.fori_loop(0, NG // UNITS[0], part0, 0)
    kv_step(2, 4)
    kv_step(1, 4)
    widen(1, 0, NK + 1)
    lax.fori_loop(0, NG // UNITS[1], part1, 0)
    kv_end()
    widen(2, 0, NK + 1)
    lax.fori_loop(0, NG // UNITS[2], part2, 0)

    loads[6].wait()
    loads[7].wait()
    outw[HW:QL] = jnp.zeros((QL - HW, C), BF16)
    for k in range(1, NG):
        for c in range(3):
            remote(
                oss[c].at[k], ors[c].at[k], o_send.at[c, k], o_recv.at[c, k], gpeer[k]
            ).wait_recv()

    def part(k):
        refs = oss if k == 0 else ors
        return jnp.concatenate([refs[c][k].astype(F32) for c in (1, 2, 0)], axis=1)

    logs = []
    for k in range(NG):
        t = (os0[0] if k == 0 else or0[k]).astype(F32)
        logs.append(t + pltpu.roll(t, 128 - 8, 1) + pltpu.roll(t, 128 - 16, 1))
    top = functools.reduce(jnp.maximum, logs)
    valid = (lane >= HD) & (lane < HD + HEADS)
    shares = [jnp.where(valid, jnp.exp2(t - top), 0.0) for t in logs]
    whole = functools.reduce(jnp.add, shares)
    inverse = 1.0 / jnp.where(valid, whole, 1.0)
    hrow = lax.broadcasted_iota(jnp.int32, (128, QL), 0)
    hcol = lax.broadcasted_iota(jnp.int32, (128, QL), 1)
    head = jnp.where(hrow < HD + 8, hrow - HD, hrow - HD - 8)
    spread = (
        (head >= 0) & (head < HEADS) & (hcol >= head * HD) & (hcol < (head + 1) * HD)
    ).astype(F32).astype(BF16)
    joined = jnp.zeros((TOK, QL), F32)
    for k in range(NG):
        w = shares[k] * inverse
        hi = w.astype(BF16).astype(F32)
        w = (hi + pltpu.roll(w - hi, 8, 1)).astype(BF16)
        joined = joined + jnp.dot(w, spread, preferred_element_type=F32) * part(k)
    hidden = inner[...] + jnp.dot(joined.astype(BF16), outw[...], preferred_element_type=F32)
    final = jnp.dot(hidden.astype(BF16), pout[...], preferred_element_type=F32)
    final = (resid[...].astype(F32) + final).astype(BF16)
    out_ref[0] = final[0:WIDTH]
    out_ref[1] = final[WIDTH:TOK]

    for c in range(3):
        for way in range(2):
            for s in range(4):
                ring[c][way][s].wait_send()
        for copy in cross[c]:
            copy.wait_send()
    for c in halos + stat_copies + owns[0] + owns[1]:
        c.wait_send()
    for k in range(1, NG):
        for c in range(3):
            remote(
                oss[c].at[k], ors[c].at[k], o_send.at[c, k], o_recv.at[c, k], gpeer[k]
            ).wait_send()
            remote(
                qs[c].at[0], qs[c].at[k], q_send.at[c, k], q_recv.at[c, k], gpeer[k]
            ).wait_send()


def hand_over(out, fresh, out_ref, fresh_ref):
    out_ref[...] = out[...]
    fresh_ref[...] = fresh[...]


def local(
    latent, gn_gain, gn_bias, conv_weight, conv_bias, attn_gain, attn_bias, proj_in, ln_gain,
    qkv_weight, out_weight, proj_out, stale_kv,
):
    hbm = pl.BlockSpec(memory_space=pl.ANY)
    vmem = pl.BlockSpec(memory_space=pltpu.VMEM)
    dma = pltpu.SemaphoreType.DMA
    done = pl.pallas_call(
        kernel,
        out_shape=(
            jax.ShapeDtypeStruct((ROWS, WIDTH, C), BF16),
            jax.ShapeDtypeStruct((TOK, 2 * HW), BF16),
        ),
        in_specs=[hbm, vmem, vmem, hbm, vmem, vmem, vmem, hbm, vmem, hbm, hbm, hbm, hbm],
        out_specs=(vmem, vmem),
        scratch_shapes=[
            pltpu.VMEM((TOK, C), BF16),
            pltpu.VMEM((2 * WIDTH, C), BF16),
            pltpu.VMEM((9 * C, C), BF16),
            pltpu.VMEM((C, C), BF16),
            pltpu.VMEM((3 * HW, C), BF16),
            pltpu.VMEM((QL, C), BF16),
            pltpu.VMEM((C, C), BF16),
            pltpu.VMEM(((NK + 1) * TOK, 128), BF16),
            pltpu.VMEM(((NK + 1) * TOK, 256), BF16),
            pltpu.VMEM(((NK + 1) * TOK, 256), BF16),
            pltpu.VMEM((TOK, 2 * HW), BF16),
            pltpu.VMEM((HEADS, (NK + 1) * TOK, 128), BF16),
            pltpu.VMEM(((ROWS + 2) * WIDTH, 3 * C), BF16),
            pltpu.VMEM((TOK, C), F32),
            pltpu.VMEM((TOK, C), BF16),
            pltpu.VMEM((TOK, C), F32),
            pltpu.VMEM((C, 128), BF16),
            pltpu.VMEM((128, C), BF16),
            pltpu.VMEM((2, 2, 8, 128), F32),
            pltpu.VMEM((2, 2, 8, 8, 128), F32),
            *[pltpu.VMEM((NG, TOK, 128), BF16)] * 3,
            pltpu.VMEM((2, TOK, KEYS), F32),
            pltpu.VMEM((NG, TOK, 128), F32),
            *[pltpu.VMEM((NG, TOK, 128), BF16)] * 6,
            dma((8,)), dma((3, 2, 4)), dma((3, 2, 4)), dma((2, 2)), dma((2, 2)), dma((3, 2, 5)), dma((3, 2, 5)), dma((2,)), dma((2,)),
            dma((2, 2, 8)), dma((2, 2, 8)), dma((3, NG)), dma((3, NG)), dma((3, NG)), dma((3, NG)),
        ],
        compiler_params=pltpu.CompilerParams(
            collective_id=0, has_side_effects=True, vmem_limit_bytes=56 * 2**20
        ),
    )(
        latent, gn_gain, gn_bias, conv_weight, conv_bias, attn_gain,
        attn_bias, proj_in, ln_gain, qkv_weight.T, out_weight, proj_out, stale_kv,
    )
    return pl.pallas_call(
        hand_over,
        out_shape=tuple(jax.ShapeDtypeStruct(v.shape, v.dtype) for v in done),
        in_specs=[vmem] * 2,
        out_specs=(vmem,) * 2,
    )(*done)


def solution(mesh):
    in_specs = (P(("req", "patch"), None, None),) + (P(),) * 11 + (P(("req", "patch"), None),)
    out_specs = (P(("req", "patch"), None, None), P(("req", "patch"), None))
    return jax.shard_map(local, mesh=mesh, in_specs=in_specs, out_specs=out_specs, check_vma=False)
```

```python
import functools

import jax
import jax.numpy as jnp
from jax import lax
from jax.experimental import pallas as pl
from jax.experimental.pallas import tpu as pltpu
from jax.sharding import PartitionSpec as P

C = 640
GROUPS = 32
PER_GROUP = C // GROUPS
HEADS = 5
HD = 64
WIDTH = 128
ROWS = 2
TOK = ROWS * WIDTH
HW = HEADS * HD
QL = 384
NY, NZ, NX = 4, 8, 2
NP = NY * NZ * NX
NG = NY
NK = NZ * NX
KEYS = NK * TOK
TILE = 1024
SCALE = (1.0 / HD**0.5) * 1.4426950408889634
F32 = jnp.float32
BF16 = jnp.bfloat16
OFFSETS = (0, 1, 3, 2)
PARTS = ((4,), (0, 1), (2, 3))
UNITS = (2, 2, 2)


def place(y, z, x):
    return (lax.rem(y + NY, NY) * NZ + lax.rem(z + NZ, NZ)) * NX + lax.rem(x + NX, NX)


def remote(src, dst, send, recv, patch):
    return pltpu.make_async_remote_copy(
        src_ref=src,
        dst_ref=dst,
        send_sem=send,
        recv_sem=recv,
        device_id={"patch": patch},
        device_id_type=pl.DeviceIdType.MESH,
    )


def kernel(
    lat_hbm, gain1, bias1, convw_hbm, convb, gain2, bias2, pin_hbm, lng, qkvw_hbm, outw_hbm,
    pout_hbm, kv_hbm,
    out_ref, fresh_ref,
    lat, halo, convw, pin, qkvw, outw, pout, kv0, kv1, kv2, own, vm, act, acc, resid, inner, gmat, gmat_t,
    stat_src, stat_buf, q0, q1, q2, sbuf, logs_ref, os0, os1, os2, or0, or1, or2,
    lsem, kv_send, kv_recv, own_send, own_recv, x_send, x_recv, h_send, h_recv, st_send, st_recv, q_send, q_recv, o_send, o_recv,
):
    p = lax.axis_index("patch")
    y, z, x = p // (NZ * NX), lax.rem(p // NX, NZ), lax.rem(p, NX)

    up, down = lax.rem(p + NP - 1, NP), lax.rem(p + 1, NP)
    zpeer = [place(y, z + d, x) for d in range(NZ)]
    gpeer = [place(y + dy, z, x) for dy in OFFSETS]
    wpeer = [place(y + k // NX, z, x + k % NX) for k in range(NY * NX)]
    barrier = pltpu.get_barrier_semaphore()
    partners = zpeer[1:] + wpeer[1:] + [up, down]
    for q in partners:
        pl.semaphore_signal(
            barrier, inc=1, device_id={"patch": q}, device_id_type=pl.DeviceIdType.MESH
        )

    loads = [
        pltpu.make_async_copy(lat_hbm.at[0], lat.at[pl.ds(0, WIDTH)], lsem.at[0]),
        pltpu.make_async_copy(lat_hbm.at[1], lat.at[pl.ds(WIDTH, WIDTH)], lsem.at[1]),
        pltpu.make_async_copy(kv_hbm, own, lsem.at[2]),
        pltpu.make_async_copy(convw_hbm, convw, lsem.at[3]),
        pltpu.make_async_copy(pin_hbm, pin, lsem.at[4]),
        pltpu.make_async_copy(qkvw_hbm, qkvw, lsem.at[5]),
        pltpu.make_async_copy(outw_hbm, outw.at[pl.ds(0, HW)], lsem.at[6]),
        pltpu.make_async_copy(pout_hbm, pout, lsem.at[7]),
    ]
    for c in loads:
        c.start()

    parts = (kv0, kv1, kv2)

    def pack(block, keys, values):
        rows = pl.ds(block * TOK, TOK)
        for c in (1, 2):
            parts[c][rows, 0:128] = keys[:, (c - 1) * 128 : c * 128]
            parts[c][rows, 128:256] = values[:, (c - 1) * 128 : c * 128]
        kv0[rows, 0:64] = keys[:, 256:320]
        kv0[rows, 64:128] = values[:, 256:320]

    loads[2].wait()
    pack(NK, own[:, 0:HW], own[:, HW : 2 * HW])

    ch = lax.broadcasted_iota(jnp.int32, (C, 128), 0)
    gr = lax.broadcasted_iota(jnp.int32, (C, 128), 1)
    gmat[...] = ((ch >= gr * PER_GROUP) & (ch < (gr + 1) * PER_GROUP)).astype(F32).astype(BF16)
    ch = lax.broadcasted_iota(jnp.int32, (128, C), 1)
    gr = lax.broadcasted_iota(jnp.int32, (128, C), 0)
    gmat_t[...] = ((ch >= gr * PER_GROUP) & (ch < (gr + 1) * PER_GROUP)).astype(F32).astype(BF16)

    def three(v, row, out):
        at = lax.broadcasted_iota(jnp.int32, out.shape, 0)
        for t in range(3):
            short = v.astype(BF16).astype(F32)
            out = jnp.where(at == row + t, short, out)
            v = v - short
        return out

    def to_groups(v):
        r = jnp.dot(
            three(v, 0, jnp.zeros((16, C), F32)).astype(BF16), gmat[...], preferred_element_type=F32
        )
        return r[0:1] + r[1:2] + r[2:3]

    def to_channels(v, w):
        r = three(w, 3, three(v, 0, jnp.zeros((16, 128), F32)))
        r = jnp.dot(r.astype(BF16), gmat_t[...], preferred_element_type=F32)
        return r[0:1] + r[1:2] + r[2:3], r[3:4] + r[4:5] + r[5:6]

    stat_copies = []

    low_groups = lax.broadcasted_iota(jnp.int32, (1, 128), 1) < GROUPS

    def local_sums(ref):
        values = ref[...].astype(F32)
        sums = to_groups(values.sum(axis=0, keepdims=True))
        middle = sums * (1.0 / (TOK * PER_GROUP))
        centred = values - to_channels(middle, middle)[0]
        return sums, to_groups((centred * centred).sum(axis=0, keepdims=True))

    def statistics(found, i, steps):
        sums, squares = found
        n = float(TOK * PER_GROUP)
        for rnd, peers in ((0, zpeer), (1, wpeer)):
            tile = jnp.where(low_groups, sums, pltpu.roll(squares, GROUPS, 1))
            stat_src[i, rnd, 0:1] = tile
            copies = [
                remote(
                    stat_src.at[i, rnd, pl.ds(0, 1)], stat_buf.at[i, rnd, k, pl.ds(0, 1)],
                    st_send.at[i, rnd, k], st_recv.at[i, rnd, k], peers[k],
                )
                for k in range(1, 8)
            ]
            for c in copies:
                c.start()
            steps[rnd]()
            for c in copies:
                c.wait_recv()
            stat_copies.extend(copies)
            parts = [tile] + [stat_buf[i, rnd, k, 0:1] for k in range(1, 8)]
            total = functools.reduce(jnp.add, parts)
            mean = total * (1.0 / (8 * n))
            spread = functools.reduce(
                jnp.add,
                [pltpu.roll(t, 128 - GROUPS, 1) + (t * (1.0 / n) - mean) ** 2 * n for t in parts],
            )
            sums = jnp.where(low_groups, total, 0.0)
            squares = jnp.where(low_groups, spread, 0.0)
            n = n * 8
        return to_channels(sums * (1.0 / n), lax.rsqrt(squares * (1.0 / n) + 1e-05))

    loads[0].wait()
    loads[1].wait()
    found = local_sums(lat)
    pl.semaphore_wait(barrier, len(partners))

    def ahead(way, s):
        if s < 0:
            return NZ
        return NZ - 1 - s if way == 0 else s + 1

    def cut(s, way, n):
        return (0, n) if s < 3 else ((0, n // 2) if way == 0 else (n // 2, n // 2))

    def rows_of(c, r, lo, n):
        return parts[c].at[pl.ds((2 * r - (c < 2)) * TOK + lo, n)]

    def kv_copy(c, way, s):
        lo, n = cut(s, way, 2 * TOK if c < 2 and s > 0 else TOK)
        return remote(
            rows_of(c, ahead(way, s - 1), lo, n), rows_of(c, ahead(way, s), lo, n),
            kv_send.at[c, way, s], kv_recv.at[c, way, s], zpeer[1] if way == 0 else zpeer[NZ - 1],
        )

    def own_copy(c, way):
        return remote(
            parts[c].at[pl.ds(2 * NZ * TOK, TOK)],
            parts[c].at[pl.ds(2 * ahead(way, 0) * TOK, TOK)],
            own_send.at[c, way], own_recv.at[c, way], zpeer[1] if way == 0 else zpeer[NZ - 1],
        )

    def across(c, way, s):
        lo, n = cut(s, way, TOK)
        at = 2 * ahead(way, s) * TOK + lo
        return remote(
            parts[c].at[pl.ds(at, n)], parts[c].at[pl.ds(at - TOK, n)],
            x_send.at[c, way, s + 1], x_recv.at[c, way, s + 1], wpeer[1],
        )

    ring = [[[kv_copy(c, way, s) for s in range(4)] for way in range(2)] for c in range(3)]
    owns = [[own_copy(c, way) for way in range(2)] for c in range(2)]
    cross = [[across(c, 0, -1)] for c in range(3)]
    cross[2] += [across(2, way, s) for s in range(4) for way in range(2)]

    def kv_step(c, s):
        if c < 2 and s == 0:
            cross[c][0].wait_recv()
        for way in range(2):
            if s > 0:
                ring[c][way][s - 1].wait_recv()
                if c < 2 and s == 1:
                    owns[c][way].wait_recv()
                if c == 2:
                    cross[c][1 + 2 * (s - 1) + way].start()
            if s < 4:
                ring[c][way][s].start()

    def kv_end():
        for copy in cross[2]:
            copy.wait_recv()

    halos = [
        remote(lat_hbm.at[1], halo.at[pl.ds(0, WIDTH)], h_send.at[0], h_recv.at[0], down),
        remote(lat_hbm.at[0], halo.at[pl.ds(WIDTH, WIDTH)], h_send.at[1], h_recv.at[1], up),
    ]
    def first_sends():
        cross[1][0].start()
        for c in owns[1] + owns[0]:
            c.start()
        kv_step(2, 0)
        cross[0][0].start()
        for c in halos:
            c.start()

    mean, rstd = statistics(found, 0, (first_sends, lambda: (kv_step(1, 0), kv_step(0, 0))))

    cross[2][0].start()

    scale = rstd * gain1[...].reshape(1, C)
    shift = bias1[...].reshape(1, C)
    col = lax.broadcasted_iota(jnp.int32, (WIDTH, C), 0)

    def activate(r):
        if r == 0:
            v = halo[0:WIDTH]
        elif r == ROWS + 1:
            v = halo[WIDTH : 2 * WIDTH]
        else:
            v = lat[(r - 1) * WIDTH : r * WIDTH]
        v = (v.astype(F32) - mean) * scale + shift
        v = v / (1.0 + jnp.exp(-v))
        if r == 0:
            v = jnp.where(p == 0, 0.0, v)
        elif r == ROWS + 1:
            v = jnp.where(p == NP - 1, 0.0, v)
        rows = pl.ds(r * WIDTH, WIDTH)
        act[rows, 0:C] = jnp.where(col == 0, 0.0, pltpu.roll(v, 1, 0)).astype(BF16)
        act[rows, C : 2 * C] = v.astype(BF16)
        act[rows, 2 * C : 3 * C] = jnp.where(
            col == WIDTH - 1, 0.0, pltpu.roll(v, WIDTH - 1, 0)
        ).astype(BF16)

    def convolve(r):
        return jnp.dot(
            act[r * WIDTH : r * WIDTH + TOK, :],
            convw[r * 3 * C : (r + 1) * 3 * C, :],
            preferred_element_type=F32,
        )

    activate(1)
    activate(2)
    loads[3].wait()
    acc[...] = convolve(1)
    kv_step(1, 1)
    for c in halos:
        c.wait_recv()
    activate(0)
    activate(3)
    acc[...] += convolve(0)
    resid[...] = (
        lat[...].astype(F32) + (acc[...] + convolve(2)) + convb[...].reshape(1, C)
    ).astype(BF16)

    kv_step(2, 1)
    mean, rstd = statistics(
        local_sums(resid), 1, (lambda: kv_step(0, 1), lambda: kv_step(1, 2))
    )
    scale = rstd * gain2[...].reshape(1, C)
    normed = ((resid[...].astype(F32) - mean) * scale + bias2[...].reshape(1, C)).astype(BF16)
    loads[4].wait()
    inner[...] = jnp.dot(normed, pin[...], preferred_element_type=F32)
    v = inner[...]
    v = v - v.mean(axis=1, keepdims=True)
    v = v * lax.rsqrt((v * v).mean(axis=1, keepdims=True) + 1e-05) * lng[...].reshape(1, C)
    loads[5].wait()
    lnorm = v.astype(BF16)

    def project(first):
        return lax.dot_general(
            lnorm, qkvw[first : first + HW], (((1,), (1,)), ((), ())), preferred_element_type=F32
        ).astype(BF16)

    qs, oss, ors = (q0, q1, q2), (os0, os1, os2), (or0, or1, or2)

    def send_queries(c, k, patch):
        remote(qs[c].at[0], qs[c].at[k], q_send.at[c, k], q_recv.at[c, k], patch).start()

    queries = project(0)
    q0[0, :, 0:64] = queries[:, 256:320]
    q0[0, :, 64:128] = jnp.zeros((TOK, 64), BF16)
    for c in (1, 2):
        qs[c][0] = queries[:, (c - 1) * 128 : c * 128]
    for c in (1, 0, 2):
        for k in range(1, NG):
            send_queries(c, k, gpeer[k])
    keys, values = project(HW), project(2 * HW)
    fresh_ref[:, 0:HW] = keys
    fresh_ref[:, HW : 2 * HW] = values
    pack(0, keys, values)

    lane = lax.broadcasted_iota(jnp.int32, (TOK, 128), 1)
    low = lane < HD

    def widen(c, first, last):
        def one(b, carry):
            rows = pl.ds(pl.multiple_of(b * TOK, TOK), TOK)
            for i, h in enumerate(PARTS[c]):
                v = parts[c][rows, 128:256] if c > 0 else kv0[rows, :]
                upper = i == 1 or c == 0
                vm[h, rows, :] = jnp.where(~low if upper else low, v.astype(F32), 1.0).astype(BF16)
            return carry

        lax.fori_loop(first, last, one, 0)

    tiles = KEYS // TILE

    def attend(c, slots, before, after):
        def begin(k):
            return pl.multiple_of(jnp.where(k == 0, 0, TOK), TOK)

        def query(k, i):
            q = qs[c][k].astype(F32)
            return jnp.where(~low if i else low, q, 0.0).astype(BF16)

        def score(q, k, t):
            keys = parts[c][pl.ds(pl.multiple_of(begin(k) + t * TILE, TOK), TILE), 0:128]
            return lax.dot_general(q, keys, (((1,), (1,)), ((), ())), preferred_element_type=F32)

        def largest(m, s):
            for j in range(TILE // 128):
                part = s[:, j * 128 : (j + 1) * 128]
                m = part if m is None else jnp.maximum(m, part)
            return m

        work = [(k, i) for k in slots for i in range(len(PARTS[c]))]
        before(0)
        q = query(*work[0])
        top = None
        for t in range(tiles):
            s = score(q, slots[0], t)
            sbuf[0, :, t * TILE : (t + 1) * TILE] = s
            top = largest(top, s)
        ratios, stats = [], None
        for n, (k, i) in enumerate(work):
            h = PARTS[c][i]
            m = jnp.max(top, axis=1, keepdims=True) * SCALE
            top = None
            o = None
            following = work[n + 1] if n + 1 < len(work) else None
            if following:
                if following[1] == 0:
                    before((n + 1) // len(PARTS[c]))
                q = query(*following)
            for t in range(tiles):
                cols = slice(t * TILE, (t + 1) * TILE)
                if following:
                    s = score(q, following[0], t)
                    sbuf[(n + 1) % 2, :, cols] = s
                    top = largest(top, s)
                w = jnp.exp2(sbuf[n % 2, :, cols] * SCALE - m).astype(BF16)
                d = jnp.dot(
                    w,
                    vm[h, pl.ds(pl.multiple_of(begin(k) + t * TILE, TOK), TILE), :],
                    preferred_element_type=F32,
                )
                o = d if o is None else o + d
            turned = pltpu.roll(o, HD, 1)
            ratio = turned / o if c == 0 else o / turned
            log = jnp.log2(turned if i == 1 or c == 0 else o) + m
            ratios.append(ratio)
            stats = jnp.where(lane == HD + h, log, 0.0 if stats is None else stats)
            if i + 1 == len(PARTS[c]):
                after(n // len(PARTS[c]), k, ratios, stats)
                ratios, stats = [], None

    def behind(k, sign):
        dy = jnp.where(k == 1, 1, jnp.where(k == 2, 3, jnp.where(k == 3, 2, 0)))
        return place(y + sign * dy, z, x)

    def give_back(c, k):
        remote(
            oss[c].at[k], ors[c].at[k], o_send.at[c, k], o_recv.at[c, k], behind(k, -1)
        ).start()

    def await_queries(c, k):
        remote(qs[c].at[0], qs[c].at[k], q_send.at[c, k], q_recv.at[c, k], gpeer[1]).wait_recv()

    def step(c, b, unit):
        slots = [b * unit + u if c < 2 else NG - 1 - (b * unit + u) for u in range(unit)]

        def before(u):
            if u > 0 if c < 2 else u + 1 < unit:
                await_queries(c, slots[u])
            else:
                pl.when(slots[u] > 0)(lambda: await_queries(c, slots[u]))

        def after(u, k, ratios, stats):
            if c == 0:
                oss[0][k] = ratios[0].astype(BF16)
                logs_ref[k] += stats
                return
            oss[c][k] = jnp.where(low, ratios[0], ratios[1]).astype(BF16)
            if c == 1:
                logs_ref[k] = stats
                return
            stats = logs_ref[k] + stats
            first = stats.astype(BF16).astype(F32)
            rest = stats - first
            second = rest.astype(BF16).astype(F32)
            third = rest - second
            tail = jnp.where(
                lane < HD + 8,
                first,
                jnp.where(lane < HD + 16, pltpu.roll(second, 8, 1), pltpu.roll(third, 16, 1)),
            )
            os0[k] = jnp.where(low, os0[k].astype(F32), tail).astype(BF16)
            if u + 1 < unit:
                give_back(2, k)
                give_back(0, k)

        attend(c, slots, before, after)
        if c > 0:
            for u in range(unit):
                if c == 1 and u > 0:
                    give_back(1, slots[u])
                elif c == 1 or u + 1 == unit:

                    @pl.when(slots[u] > 0)
                    def _():
                        give_back(c, slots[u])
                        if c == 2:
                            give_back(0, slots[u])

    kv_step(1, 3)
    kv_step(2, 2)
    kv_step(0, 2)
    kv_step(1, 4)
    widen(1, 0, NK + 1)

    def part1(b, carry):
        pl.when(b == 1)(lambda: (kv_step(0, 3), kv_step(2, 3)) and None)
        step(1, b, UNITS[1])
        return carry

    def part0(b, carry):
        step(0, b, UNITS[0])
        return carry

    def part2(b, carry):
        step(2, b, UNITS[2])
        return carry

    lax.fori_loop(0, NG // UNITS[1], part1, 0)
    kv_step(0, 4)
    kv_step(2, 4)
    widen(0, 0, NK + 1)
    lax.fori_loop(0, NG // UNITS[0], part0, 0)
    kv_end()
    widen(2, 0, NK + 1)
    lax.fori_loop(0, NG // UNITS[2], part2, 0)

    loads[6].wait()
    loads[7].wait()
    outw[HW:QL] = jnp.zeros((QL - HW, C), BF16)
    for k in range(1, NG):
        for c in range(3):
            remote(
                oss[c].at[k], ors[c].at[k], o_send.at[c, k], o_recv.at[c, k], gpeer[k]
            ).wait_recv()

    def part(k):
        refs = oss if k == 0 else ors
        return jnp.concatenate([refs[c][k].astype(F32) for c in (1, 2, 0)], axis=1)

    logs = []
    for k in range(NG):
        t = (os0[0] if k == 0 else or0[k]).astype(F32)
        logs.append(t + pltpu.roll(t, 128 - 8, 1) + pltpu.roll(t, 128 - 16, 1))
    top = functools.reduce(jnp.maximum, logs)
    valid = (lane >= HD) & (lane < HD + HEADS)
    shares = [jnp.where(valid, jnp.exp2(t - top), 0.0) for t in logs]
    whole = functools.reduce(jnp.add, shares)
    inverse = 1.0 / jnp.where(valid, whole, 1.0)
    hrow = lax.broadcasted_iota(jnp.int32, (128, QL), 0)
    hcol = lax.broadcasted_iota(jnp.int32, (128, QL), 1)
    head = jnp.where(hrow < HD + 8, hrow - HD, hrow - HD - 8)
    spread = (
        (head >= 0) & (head < HEADS) & (hcol >= head * HD) & (hcol < (head + 1) * HD)
    ).astype(F32).astype(BF16)
    joined = jnp.zeros((TOK, QL), F32)
    for k in range(NG):
        w = shares[k] * inverse
        hi = w.astype(BF16).astype(F32)
        w = (hi + pltpu.roll(w - hi, 8, 1)).astype(BF16)
        joined = joined + jnp.dot(w, spread, preferred_element_type=F32) * part(k)
    hidden = inner[...] + jnp.dot(joined.astype(BF16), outw[...], preferred_element_type=F32)
    final = jnp.dot(hidden.astype(BF16), pout[...], preferred_element_type=F32)
    final = (resid[...].astype(F32) + final).astype(BF16)
    out_ref[0] = final[0:WIDTH]
    out_ref[1] = final[WIDTH:TOK]

    for c in range(3):
        for way in range(2):
            for s in range(4):
                ring[c][way][s].wait_send()
        for copy in cross[c]:
            copy.wait_send()
    for c in halos + stat_copies + owns[0] + owns[1]:
        c.wait_send()
    for k in range(1, NG):
        for c in range(3):
            remote(
                oss[c].at[k], ors[c].at[k], o_send.at[c, k], o_recv.at[c, k], gpeer[k]
            ).wait_send()
            remote(
                qs[c].at[0], qs[c].at[k], q_send.at[c, k], q_recv.at[c, k], gpeer[k]
            ).wait_send()


def hand_over(out, fresh, out_ref, fresh_ref):
    out_ref[...] = out[...]
    fresh_ref[...] = fresh[...]


def local(
    latent, gn_gain, gn_bias, conv_weight, conv_bias, attn_gain, attn_bias, proj_in, ln_gain,
    qkv_weight, out_weight, proj_out, stale_kv,
):
    hbm = pl.BlockSpec(memory_space=pl.ANY)
    vmem = pl.BlockSpec(memory_space=pltpu.VMEM)
    dma = pltpu.SemaphoreType.DMA
    done = pl.pallas_call(
        kernel,
        out_shape=(
            jax.ShapeDtypeStruct((ROWS, WIDTH, C), BF16),
            jax.ShapeDtypeStruct((TOK, 2 * HW), BF16),
        ),
        in_specs=[hbm, vmem, vmem, hbm, vmem, vmem, vmem, hbm, vmem, hbm, hbm, hbm, hbm],
        out_specs=(vmem, vmem),
        scratch_shapes=[
            pltpu.VMEM((TOK, C), BF16),
            pltpu.VMEM((2 * WIDTH, C), BF16),
            pltpu.VMEM((9 * C, C), BF16),
            pltpu.VMEM((C, C), BF16),
            pltpu.VMEM((3 * HW, C), BF16),
            pltpu.VMEM((QL, C), BF16),
            pltpu.VMEM((C, C), BF16),
            pltpu.VMEM(((NK + 1) * TOK, 128), BF16),
            pltpu.VMEM(((NK + 1) * TOK, 256), BF16),
            pltpu.VMEM(((NK + 1) * TOK, 256), BF16),
            pltpu.VMEM((TOK, 2 * HW), BF16),
            pltpu.VMEM((HEADS, (NK + 1) * TOK, 128), BF16),
            pltpu.VMEM(((ROWS + 2) * WIDTH, 3 * C), BF16),
            pltpu.VMEM((TOK, C), F32),
            pltpu.VMEM((TOK, C), BF16),
            pltpu.VMEM((TOK, C), F32),
            pltpu.VMEM((C, 128), BF16),
            pltpu.VMEM((128, C), BF16),
            pltpu.VMEM((2, 2, 8, 128), F32),
            pltpu.VMEM((2, 2, 8, 8, 128), F32),
            *[pltpu.VMEM((NG, TOK, 128), BF16)] * 3,
            pltpu.VMEM((2, TOK, KEYS), F32),
            pltpu.VMEM((NG, TOK, 128), F32),
            *[pltpu.VMEM((NG, TOK, 128), BF16)] * 6,
            dma((8,)), dma((3, 2, 4)), dma((3, 2, 4)), dma((2, 2)), dma((2, 2)), dma((3, 2, 5)), dma((3, 2, 5)), dma((2,)), dma((2,)),
            dma((2, 2, 8)), dma((2, 2, 8)), dma((3, NG)), dma((3, NG)), dma((3, NG)), dma((3, NG)),
        ],
        compiler_params=pltpu.CompilerParams(
            collective_id=0, has_side_effects=True, vmem_limit_bytes=56 * 2**20
        ),
    )(
        latent, gn_gain, gn_bias, conv_weight, conv_bias, attn_gain,
        attn_bias, proj_in, ln_gain, qkv_weight.T, out_weight, proj_out, stale_kv,
    )
    return pl.pallas_call(
        hand_over,
        out_shape=tuple(jax.ShapeDtypeStruct(v.shape, v.dtype) for v in done),
        in_specs=[vmem] * 2,
        out_specs=(vmem,) * 2,
    )(*done)


def solution(mesh):
    in_specs = (P(("req", "patch"), None, None),) + (P(),) * 11 + (P(("req", "patch"), None),)
    out_specs = (P(("req", "patch"), None, None), P(("req", "patch"), None))
    return jax.shard_map(local, mesh=mesh, in_specs=in_specs, out_specs=out_specs, check_vma=False)
```

```python
import functools

import jax
import jax.numpy as jnp
from jax import lax
from jax.experimental import pallas as pl
from jax.experimental.pallas import tpu as pltpu
from jax.sharding import PartitionSpec as P

C = 640
GROUPS = 32
PER_GROUP = C // GROUPS
HEADS = 5
HD = 64
WIDTH = 128
ROWS = 2
TOK = ROWS * WIDTH
HW = HEADS * HD
QL = 384
NY, NZ, NX = 4, 8, 2
NP = NY * NZ * NX
NG = NY
NK = NZ * NX
KEYS = NK * TOK
TILE = 1024
SCALE = (1.0 / HD**0.5) * 1.4426950408889634
F32 = jnp.float32
BF16 = jnp.bfloat16
OFFSETS = (0, 1, 3, 2)
PARTS = ((4,), (0, 1), (2, 3))
UNITS = (2, 2, 2)


def place(y, z, x):
    return (lax.rem(y + NY, NY) * NZ + lax.rem(z + NZ, NZ)) * NX + lax.rem(x + NX, NX)


def remote(src, dst, send, recv, patch):
    return pltpu.make_async_remote_copy(
        src_ref=src,
        dst_ref=dst,
        send_sem=send,
        recv_sem=recv,
        device_id={"patch": patch},
        device_id_type=pl.DeviceIdType.MESH,
    )


def kernel(
    lat_hbm, gain1, bias1, convw_hbm, convb, gain2, bias2, pin_hbm, lng, qkvw_hbm, outw_hbm,
    pout_hbm, kv_hbm,
    out_ref, fresh_ref,
    lat, halo, convw, pin, qkvw, outw, pout, kv0, kv1, kv2, own, vm, act, acc, resid, inner, gmat, gmat_t,
    stat_src, stat_buf, q0, q1, q2, sbuf, logs_ref, os0, os1, os2, or0, or1, or2,
    lsem, kv_send, kv_recv, own_send, own_recv, x_send, x_recv, h_send, h_recv, st_send, st_recv, q_send, q_recv, o_send, o_recv,
):
    p = lax.axis_index("patch")
    y, z, x = p // (NZ * NX), lax.rem(p // NX, NZ), lax.rem(p, NX)

    up, down = lax.rem(p + NP - 1, NP), lax.rem(p + 1, NP)
    zpeer = [place(y, z + d, x) for d in range(NZ)]
    gpeer = [place(y + dy, z, x) for dy in OFFSETS]
    wpeer = [place(y + k // NX, z, x + k % NX) for k in range(NY * NX)]
    barrier = pltpu.get_barrier_semaphore()
    partners = zpeer[1:] + wpeer[1:] + [up, down]
    for q in partners:
        pl.semaphore_signal(
            barrier, inc=1, device_id={"patch": q}, device_id_type=pl.DeviceIdType.MESH
        )

    loads = [
        pltpu.make_async_copy(lat_hbm.at[0], lat.at[pl.ds(0, WIDTH)], lsem.at[0]),
        pltpu.make_async_copy(lat_hbm.at[1], lat.at[pl.ds(WIDTH, WIDTH)], lsem.at[1]),
        pltpu.make_async_copy(kv_hbm, own, lsem.at[2]),
        pltpu.make_async_copy(convw_hbm, convw, lsem.at[3]),
        pltpu.make_async_copy(pin_hbm, pin, lsem.at[4]),
        pltpu.make_async_copy(qkvw_hbm, qkvw, lsem.at[5]),
        pltpu.make_async_copy(outw_hbm, outw.at[pl.ds(0, HW)], lsem.at[6]),
        pltpu.make_async_copy(pout_hbm, pout, lsem.at[7]),
    ]
    for c in loads:
        c.start()

    parts = (kv0, kv1, kv2)

    def pack(block, keys, values):
        rows = pl.ds(block * TOK, TOK)
        for c in (1, 2):
            parts[c][rows, 0:128] = keys[:, (c - 1) * 128 : c * 128]
            parts[c][rows, 128:256] = values[:, (c - 1) * 128 : c * 128]
        kv0[rows, 0:64] = keys[:, 256:320]
        kv0[rows, 64:128] = values[:, 256:320]

    loads[2].wait()
    pack(NK, own[:, 0:HW], own[:, HW : 2 * HW])

    ch = lax.broadcasted_iota(jnp.int32, (C, 128), 0)
    gr = lax.broadcasted_iota(jnp.int32, (C, 128), 1)
    gmat[...] = ((ch >= gr * PER_GROUP) & (ch < (gr + 1) * PER_GROUP)).astype(F32).astype(BF16)
    ch = lax.broadcasted_iota(jnp.int32, (128, C), 1)
    gr = lax.broadcasted_iota(jnp.int32, (128, C), 0)
    gmat_t[...] = ((ch >= gr * PER_GROUP) & (ch < (gr + 1) * PER_GROUP)).astype(F32).astype(BF16)

    def three(v, row, out):
        at = lax.broadcasted_iota(jnp.int32, out.shape, 0)
        for t in range(3):
            short = v.astype(BF16).astype(F32)
            out = jnp.where(at == row + t, short, out)
            v = v - short
        return out

    def to_groups(v):
        r = jnp.dot(
            three(v, 0, jnp.zeros((16, C), F32)).astype(BF16), gmat[...], preferred_element_type=F32
        )
        return r[0:1] + r[1:2] + r[2:3]

    def to_channels(v, w):
        r = three(w, 3, three(v, 0, jnp.zeros((16, 128), F32)))
        r = jnp.dot(r.astype(BF16), gmat_t[...], preferred_element_type=F32)
        return r[0:1] + r[1:2] + r[2:3], r[3:4] + r[4:5] + r[5:6]

    stat_copies = []

    low_groups = lax.broadcasted_iota(jnp.int32, (1, 128), 1) < GROUPS

    def local_sums(ref):
        values = ref[...].astype(F32)
        sums = to_groups(values.sum(axis=0, keepdims=True))
        middle = sums * (1.0 / (TOK * PER_GROUP))
        centred = values - to_channels(middle, middle)[0]
        return sums, to_groups((centred * centred).sum(axis=0, keepdims=True))

    def statistics(found, i, steps):
        sums, squares = found
        n = float(TOK * PER_GROUP)
        for rnd, peers in enumerate((zpeer, wpeer) if i == 0 else (wpeer, zpeer)):
            tile = jnp.where(low_groups, sums, pltpu.roll(squares, GROUPS, 1))
            stat_src[i, rnd, 0:1] = tile
            copies = [
                remote(
                    stat_src.at[i, rnd, pl.ds(0, 1)], stat_buf.at[i, rnd, k, pl.ds(0, 1)],
                    st_send.at[i, rnd, k], st_recv.at[i, rnd, k], peers[k],
                )
                for k in range(1, 8)
            ]
            for c in copies:
                c.start()
            steps[rnd]()
            for c in copies:
                c.wait_recv()
            stat_copies.extend(copies)
            parts = [tile] + [stat_buf[i, rnd, k, 0:1] for k in range(1, 8)]
            total = functools.reduce(jnp.add, parts)
            mean = total * (1.0 / (8 * n))
            spread = functools.reduce(
                jnp.add,
                [pltpu.roll(t, 128 - GROUPS, 1) + (t * (1.0 / n) - mean) ** 2 * n for t in parts],
            )
            sums = jnp.where(low_groups, total, 0.0)
            squares = jnp.where(low_groups, spread, 0.0)
            n = n * 8
        return to_channels(sums * (1.0 / n), lax.rsqrt(squares * (1.0 / n) + 1e-05))

    loads[0].wait()
    loads[1].wait()
    found = local_sums(lat)
    pl.semaphore_wait(barrier, len(partners))

    def ahead(way, s):
        if s < 0:
            return NZ
        return NZ - 1 - s if way == 0 else s + 1

    def cut(s, way, n):
        return (0, n) if s < 3 else ((0, n // 2) if way == 0 else (n // 2, n // 2))

    def rows_of(c, r, lo, n):
        return parts[c].at[pl.ds((2 * r - (c < 2)) * TOK + lo, n)]

    def kv_copy(c, way, s):
        lo, n = cut(s, way, 2 * TOK if c < 2 and s > 0 else TOK)
        return remote(
            rows_of(c, ahead(way, s - 1), lo, n), rows_of(c, ahead(way, s), lo, n),
            kv_send.at[c, way, s], kv_recv.at[c, way, s], zpeer[1] if way == 0 else zpeer[NZ - 1],
        )

    def own_copy(c, way):
        return remote(
            parts[c].at[pl.ds(2 * NZ * TOK, TOK)],
            parts[c].at[pl.ds(2 * ahead(way, 0) * TOK, TOK)],
            own_send.at[c, way], own_recv.at[c, way], zpeer[1] if way == 0 else zpeer[NZ - 1],
        )

    def across(c, way, s):
        lo, n = cut(s, way, TOK)
        at = 2 * ahead(way, s) * TOK + lo
        return remote(
            parts[c].at[pl.ds(at, n)], parts[c].at[pl.ds(at - TOK, n)],
            x_send.at[c, way, s + 1], x_recv.at[c, way, s + 1], wpeer[1],
        )

    ring = [[[kv_copy(c, way, s) for s in range(4)] for way in range(2)] for c in range(3)]
    owns = [[own_copy(c, way) for way in range(2)] for c in range(2)]
    cross = [[across(c, 0, -1)] for c in range(3)]
    cross[2] += [across(2, way, s) for s in range(4) for way in range(2)]

    def kv_step(c, s):
        if c < 2 and s == 0:
            cross[c][0].wait_recv()
        for way in range(2):
            if s > 0:
                ring[c][way][s - 1].wait_recv()
                if c < 2 and s == 1:
                    owns[c][way].wait_recv()
                if c == 2:
                    cross[c][1 + 2 * (s - 1) + way].start()
            if s < 4:
                ring[c][way][s].start()

    def kv_end():
        for copy in cross[2]:
            copy.wait_recv()

    halos = [
        remote(lat_hbm.at[1], halo.at[pl.ds(0, WIDTH)], h_send.at[0], h_recv.at[0], down),
        remote(lat_hbm.at[0], halo.at[pl.ds(WIDTH, WIDTH)], h_send.at[1], h_recv.at[1], up),
    ]
    def first_sends():
        cross[1][0].start()
        for c in owns[1] + owns[0]:
            c.start()
        kv_step(2, 0)
        cross[0][0].start()
        for c in halos:
            c.start()

    mean, rstd = statistics(found, 0, (first_sends, lambda: (kv_step(1, 0), kv_step(0, 0))))

    cross[2][0].start()

    scale = rstd * gain1[...].reshape(1, C)
    shift = bias1[...].reshape(1, C)
    col = lax.broadcasted_iota(jnp.int32, (WIDTH, C), 0)

    def activate(r):
        if r == 0:
            v = halo[0:WIDTH]
        elif r == ROWS + 1:
            v = halo[WIDTH : 2 * WIDTH]
        else:
            v = lat[(r - 1) * WIDTH : r * WIDTH]
        v = (v.astype(F32) - mean) * scale + shift
        v = v / (1.0 + jnp.exp(-v))
        if r == 0:
            v = jnp.where(p == 0, 0.0, v)
        elif r == ROWS + 1:
            v = jnp.where(p == NP - 1, 0.0, v)
        rows = pl.ds(r * WIDTH, WIDTH)
        act[rows, 0:C] = jnp.where(col == 0, 0.0, pltpu.roll(v, 1, 0)).astype(BF16)
        act[rows, C : 2 * C] = v.astype(BF16)
        act[rows, 2 * C : 3 * C] = jnp.where(
            col == WIDTH - 1, 0.0, pltpu.roll(v, WIDTH - 1, 0)
        ).astype(BF16)

    def convolve(r):
        return jnp.dot(
            act[r * WIDTH : r * WIDTH + TOK, :],
            convw[r * 3 * C : (r + 1) * 3 * C, :],
            preferred_element_type=F32,
        )

    activate(1)
    activate(2)
    loads[3].wait()
    acc[...] = convolve(1)
    kv_step(1, 1)
    for c in halos:
        c.wait_recv()
    activate(0)
    activate(3)
    acc[...] += convolve(0)
    resid[...] = (
        lat[...].astype(F32) + (acc[...] + convolve(2)) + convb[...].reshape(1, C)
    ).astype(BF16)

    kv_step(2, 1)
    mean, rstd = statistics(
        local_sums(resid), 1, (lambda: kv_step(0, 1), lambda: kv_step(1, 2))
    )
    scale = rstd * gain2[...].reshape(1, C)
    normed = ((resid[...].astype(F32) - mean) * scale + bias2[...].reshape(1, C)).astype(BF16)
    loads[4].wait()
    inner[...] = jnp.dot(normed, pin[...], preferred_element_type=F32)
    v = inner[...]
    v = v - v.mean(axis=1, keepdims=True)
    v = v * lax.rsqrt((v * v).mean(axis=1, keepdims=True) + 1e-05) * lng[...].reshape(1, C)
    loads[5].wait()
    lnorm = v.astype(BF16)

    def project(first):
        return lax.dot_general(
            lnorm, qkvw[first : first + HW], (((1,), (1,)), ((), ())), preferred_element_type=F32
        ).astype(BF16)

    qs, oss, ors = (q0, q1, q2), (os0, os1, os2), (or0, or1, or2)

    def send_queries(c, k, patch):
        remote(qs[c].at[0], qs[c].at[k], q_send.at[c, k], q_recv.at[c, k], patch).start()

    queries = project(0)
    q0[0, :, 0:64] = queries[:, 256:320]
    q0[0, :, 64:128] = jnp.zeros((TOK, 64), BF16)
    for c in (1, 2):
        qs[c][0] = queries[:, (c - 1) * 128 : c * 128]
    for c in (1, 0, 2):
        for k in range(1, NG):
            send_queries(c, k, gpeer[k])
    keys, values = project(HW), project(2 * HW)
    fresh_ref[:, 0:HW] = keys
    fresh_ref[:, HW : 2 * HW] = values
    pack(0, keys, values)

    lane = lax.broadcasted_iota(jnp.int32, (TOK, 128), 1)
    low = lane < HD

    def widen(c, first, last):
        def one(b, carry):
            rows = pl.ds(pl.multiple_of(b * TOK, TOK), TOK)
            for i, h in enumerate(PARTS[c]):
                v = parts[c][rows, 128:256] if c > 0 else kv0[rows, :]
                upper = i == 1 or c == 0
                vm[h, rows, :] = jnp.where(~low if upper else low, v.astype(F32), 1.0).astype(BF16)
            return carry

        lax.fori_loop(first, last, one, 0)

    tiles = KEYS // TILE

    def attend(c, slots, before, after):
        def begin(k):
            return pl.multiple_of(jnp.where(k == 0, 0, TOK), TOK)

        def query(k, i):
            q = qs[c][k].astype(F32)
            return jnp.where(~low if i else low, q, 0.0).astype(BF16)

        def score(q, k, t):
            keys = parts[c][pl.ds(pl.multiple_of(begin(k) + t * TILE, TOK), TILE), 0:128]
            return lax.dot_general(q, keys, (((1,), (1,)), ((), ())), preferred_element_type=F32)

        def largest(m, s):
            for j in range(TILE // 128):
                part = s[:, j * 128 : (j + 1) * 128]
                m = part if m is None else jnp.maximum(m, part)
            return m

        work = [(k, i) for k in slots for i in range(len(PARTS[c]))]
        before(0)
        q = query(*work[0])
        top = None
        for t in range(tiles):
            s = score(q, slots[0], t)
            sbuf[0, :, t * TILE : (t + 1) * TILE] = s
            top = largest(top, s)
        ratios, stats = [], None
        for n, (k, i) in enumerate(work):
            h = PARTS[c][i]
            m = jnp.max(top, axis=1, keepdims=True) * SCALE
            top = None
            o = None
            following = work[n + 1] if n + 1 < len(work) else None
            if following:
                if following[1] == 0:
                    before((n + 1) // len(PARTS[c]))
                q = query(*following)
            for t in range(tiles):
                cols = slice(t * TILE, (t + 1) * TILE)
                if following:
                    s = score(q, following[0], t)
                    sbuf[(n + 1) % 2, :, cols] = s
                    top = largest(top, s)
                w = jnp.exp2(sbuf[n % 2, :, cols] * SCALE - m).astype(BF16)
                d = jnp.dot(
                    w,
                    vm[h, pl.ds(pl.multiple_of(begin(k) + t * TILE, TOK), TILE), :],
                    preferred_element_type=F32,
                )
                o = d if o is None else o + d
            turned = pltpu.roll(o, HD, 1)
            ratio = turned / o if c == 0 else o / turned
            log = jnp.log2(turned if i == 1 or c == 0 else o) + m
            ratios.append(ratio)
            stats = jnp.where(lane == HD + h, log, 0.0 if stats is None else stats)
            if i + 1 == len(PARTS[c]):
                after(n // len(PARTS[c]), k, ratios, stats)
                ratios, stats = [], None

    def behind(k, sign):
        dy = jnp.where(k == 1, 1, jnp.where(k == 2, 3, jnp.where(k == 3, 2, 0)))
        return place(y + sign * dy, z, x)

    def give_back(c, k):
        remote(
            oss[c].at[k], ors[c].at[k], o_send.at[c, k], o_recv.at[c, k], behind(k, -1)
        ).start()

    def await_queries(c, k):
        remote(qs[c].at[0], qs[c].at[k], q_send.at[c, k], q_recv.at[c, k], gpeer[1]).wait_recv()

    def step(c, b, unit):
        slots = [b * unit + u if c < 2 else NG - 1 - (b * unit + u) for u in range(unit)]

        def before(u):
            if u > 0 if c < 2 else u + 1 < unit:
                await_queries(c, slots[u])
            else:
                pl.when(slots[u] > 0)(lambda: await_queries(c, slots[u]))

        def after(u, k, ratios, stats):
            if c == 0:
                oss[0][k] = ratios[0].astype(BF16)
                logs_ref[k] += stats
                return
            oss[c][k] = jnp.where(low, ratios[0], ratios[1]).astype(BF16)
            if c == 1:
                logs_ref[k] = stats
                return
            stats = logs_ref[k] + stats
            first = stats.astype(BF16).astype(F32)
            rest = stats - first
            second = rest.astype(BF16).astype(F32)
            third = rest - second
            tail = jnp.where(
                lane < HD + 8,
                first,
                jnp.where(lane < HD + 16, pltpu.roll(second, 8, 1), pltpu.roll(third, 16, 1)),
            )
            os0[k] = jnp.where(low, os0[k].astype(F32), tail).astype(BF16)
            if u + 1 < unit:
                give_back(2, k)
                give_back(0, k)

        attend(c, slots, before, after)
        if c > 0:
            for u in range(unit):
                if c == 1 and u > 0:
                    give_back(1, slots[u])
                elif c == 1 or u + 1 == unit:

                    @pl.when(slots[u] > 0)
                    def _():
                        give_back(c, slots[u])
                        if c == 2:
                            give_back(0, slots[u])

    kv_step(1, 3)
    kv_step(2, 2)
    kv_step(0, 2)
    kv_step(1, 4)
    widen(1, 0, NK + 1)

    def part1(b, carry):
        pl.when(b == 1)(lambda: (kv_step(0, 3), kv_step(2, 3)) and None)
        step(1, b, UNITS[1])
        return carry

    def part0(b, carry):
        step(0, b, UNITS[0])
        return carry

    def part2(b, carry):
        step(2, b, UNITS[2])
        return carry

    lax.fori_loop(0, NG // UNITS[1], part1, 0)
    kv_step(0, 4)
    kv_step(2, 4)
    widen(0, 0, NK + 1)
    lax.fori_loop(0, NG // UNITS[0], part0, 0)
    kv_end()
    widen(2, 0, NK + 1)
    lax.fori_loop(0, NG // UNITS[2], part2, 0)

    loads[6].wait()
    loads[7].wait()
    outw[HW:QL] = jnp.zeros((QL - HW, C), BF16)
    for k in range(1, NG):
        for c in range(3):
            remote(
                oss[c].at[k], ors[c].at[k], o_send.at[c, k], o_recv.at[c, k], gpeer[k]
            ).wait_recv()

    def part(k):
        refs = oss if k == 0 else ors
        return jnp.concatenate([refs[c][k].astype(F32) for c in (1, 2, 0)], axis=1)

    logs = []
    for k in range(NG):
        t = (os0[0] if k == 0 else or0[k]).astype(F32)
        logs.append(t + pltpu.roll(t, 128 - 8, 1) + pltpu.roll(t, 128 - 16, 1))
    top = functools.reduce(jnp.maximum, logs)
    valid = (lane >= HD) & (lane < HD + HEADS)
    shares = [jnp.where(valid, jnp.exp2(t - top), 0.0) for t in logs]
    whole = functools.reduce(jnp.add, shares)
    inverse = 1.0 / jnp.where(valid, whole, 1.0)
    hrow = lax.broadcasted_iota(jnp.int32, (128, QL), 0)
    hcol = lax.broadcasted_iota(jnp.int32, (128, QL), 1)
    head = jnp.where(hrow < HD + 8, hrow - HD, hrow - HD - 8)
    spread = (
        (head >= 0) & (head < HEADS) & (hcol >= head * HD) & (hcol < (head + 1) * HD)
    ).astype(F32).astype(BF16)
    joined = jnp.zeros((TOK, QL), F32)
    for k in range(NG):
        w = shares[k] * inverse
        hi = w.astype(BF16).astype(F32)
        w = (hi + pltpu.roll(w - hi, 8, 1)).astype(BF16)
        joined = joined + jnp.dot(w, spread, preferred_element_type=F32) * part(k)
    hidden = inner[...] + jnp.dot(joined.astype(BF16), outw[...], preferred_element_type=F32)
    final = jnp.dot(hidden.astype(BF16), pout[...], preferred_element_type=F32)
    final = (resid[...].astype(F32) + final).astype(BF16)
    out_ref[0] = final[0:WIDTH]
    out_ref[1] = final[WIDTH:TOK]

    for c in range(3):
        for way in range(2):
            for s in range(4):
                ring[c][way][s].wait_send()
        for copy in cross[c]:
            copy.wait_send()
    for c in halos + stat_copies + owns[0] + owns[1]:
        c.wait_send()
    for k in range(1, NG):
        for c in range(3):
            remote(
                oss[c].at[k], ors[c].at[k], o_send.at[c, k], o_recv.at[c, k], gpeer[k]
            ).wait_send()
            remote(
                qs[c].at[0], qs[c].at[k], q_send.at[c, k], q_recv.at[c, k], gpeer[k]
            ).wait_send()


def hand_over(out, fresh, out_ref, fresh_ref):
    out_ref[...] = out[...]
    fresh_ref[...] = fresh[...]


def local(
    latent, gn_gain, gn_bias, conv_weight, conv_bias, attn_gain, attn_bias, proj_in, ln_gain,
    qkv_weight, out_weight, proj_out, stale_kv,
):
    hbm = pl.BlockSpec(memory_space=pl.ANY)
    vmem = pl.BlockSpec(memory_space=pltpu.VMEM)
    dma = pltpu.SemaphoreType.DMA
    done = pl.pallas_call(
        kernel,
        out_shape=(
            jax.ShapeDtypeStruct((ROWS, WIDTH, C), BF16),
            jax.ShapeDtypeStruct((TOK, 2 * HW), BF16),
        ),
        in_specs=[hbm, vmem, vmem, hbm, vmem, vmem, vmem, hbm, vmem, hbm, hbm, hbm, hbm],
        out_specs=(vmem, vmem),
        scratch_shapes=[
            pltpu.VMEM((TOK, C), BF16),
            pltpu.VMEM((2 * WIDTH, C), BF16),
            pltpu.VMEM((9 * C, C), BF16),
            pltpu.VMEM((C, C), BF16),
            pltpu.VMEM((3 * HW, C), BF16),
            pltpu.VMEM((QL, C), BF16),
            pltpu.VMEM((C, C), BF16),
            pltpu.VMEM(((NK + 1) * TOK, 128), BF16),
            pltpu.VMEM(((NK + 1) * TOK, 256), BF16),
            pltpu.VMEM(((NK + 1) * TOK, 256), BF16),
            pltpu.VMEM((TOK, 2 * HW), BF16),
            pltpu.VMEM((HEADS, (NK + 1) * TOK, 128), BF16),
            pltpu.VMEM(((ROWS + 2) * WIDTH, 3 * C), BF16),
            pltpu.VMEM((TOK, C), F32),
            pltpu.VMEM((TOK, C), BF16),
            pltpu.VMEM((TOK, C), F32),
            pltpu.VMEM((C, 128), BF16),
            pltpu.VMEM((128, C), BF16),
            pltpu.VMEM((2, 2, 8, 128), F32),
            pltpu.VMEM((2, 2, 8, 8, 128), F32),
            *[pltpu.VMEM((NG, TOK, 128), BF16)] * 3,
            pltpu.VMEM((2, TOK, KEYS), F32),
            pltpu.VMEM((NG, TOK, 128), F32),
            *[pltpu.VMEM((NG, TOK, 128), BF16)] * 6,
            dma((8,)), dma((3, 2, 4)), dma((3, 2, 4)), dma((2, 2)), dma((2, 2)), dma((3, 2, 5)), dma((3, 2, 5)), dma((2,)), dma((2,)),
            dma((2, 2, 8)), dma((2, 2, 8)), dma((3, NG)), dma((3, NG)), dma((3, NG)), dma((3, NG)),
        ],
        compiler_params=pltpu.CompilerParams(
            collective_id=0, has_side_effects=True, vmem_limit_bytes=56 * 2**20
        ),
    )(
        latent, gn_gain, gn_bias, conv_weight, conv_bias, attn_gain,
        attn_bias, proj_in, ln_gain, qkv_weight.T, out_weight, proj_out, stale_kv,
    )
    return pl.pallas_call(
        hand_over,
        out_shape=tuple(jax.ShapeDtypeStruct(v.shape, v.dtype) for v in done),
        in_specs=[vmem] * 2,
        out_specs=(vmem,) * 2,
    )(*done)


def solution(mesh):
    in_specs = (P(("req", "patch"), None, None),) + (P(),) * 11 + (P(("req", "patch"), None),)
    out_specs = (P(("req", "patch"), None, None), P(("req", "patch"), None))
    return jax.shard_map(local, mesh=mesh, in_specs=in_specs, out_specs=out_specs, check_vma=False)
```
